256 devices in a mesh: dp: 32 (over y_lo, z, core), seq: 8 (over x, y_hi).
Axes of the slice: x: 4, y: 4 (y_hi: 2, y_lo: 2; y = y_hi * 2 + y_lo), z: 8, core: 2. Of those that a mesh axis runs over, the one named last changes fastest.
Arguments:
- text_context: bfloat16 [32, 128, 4096], P('dp', None, 'seq'), may hold values from -6 to 6
- text_residual: bfloat16 [32, 128, 4096], P('dp'), may hold values from -6 to 6
- text_out_weight: bfloat16 [4096, 4096], P('seq'), may hold values from -0.09375 to 0.09375
- text_gain: float32 [4096], replicated, may hold values from 0.1 to 1.9
- prompt_length: int32 [32], P('dp'), may hold values from 16 to 128, as said below
- key_weight: bfloat16 [4096, 3072], P('dp', 'seq'), may hold values from -0.09375 to 0.09375
- value_weight: bfloat16 [4096, 3072], P('dp', 'seq'), may hold values from -0.09375 to 0.09375
- video_query: bfloat16 [32, 1024, 3072], P('dp', 'seq'), may hold values from -100 to 100
- video_key: bfloat16 [32, 1024, 3072], P('dp', 'seq'), may hold values from -5.05 to 5.05
- video_value: bfloat16 [32, 1024, 3072], P('dp', 'seq'), may hold values from -6 to 6
- out_cotangent: bfloat16 [32, 1024, 3072], P('dp', 'seq'), may hold values from -6 to 6
Outputs:
- attended: bfloat16 [32, 1024, 3072], P('dp', 'seq')
- query_grad: bfloat16 [32, 1024, 3072], P('dp', 'seq')
- key_grad: bfloat16 [32, 1024, 3072], P('dp', 'seq')
- value_grad: bfloat16 [32, 1024, 3072], P('dp', 'seq')
- key_weight_grad: float32 [4096, 3072], P('dp', 'seq')
- value_weight_grad: float32 [4096, 3072], P('dp', 'seq')
The draws below stay inside these ranges and needn't reach their ends.
Inputs may be any that keep to these rules, and one draw needn't show every extreme that they name: `prompt_length`: prompt slots from a clip's length on are padding; some clip of every draw has 128.
All inputs are finite; a program needn't handle non-finite values.
Results may differ from the reference program's by a relative error of at most 0.034.
Values may be sent and summed in bfloat16 or wider, within the bound.
A program may use at most 128 MiB of HBM per device.

```python
import math
import jax
import jax.numpy as jnp
from jax import lax

D_TEXT = 4096
HEADS = 24
HEAD_DIM = 128
PROMPT = 128
CLIPS = 32
TOKENS = 1024


def video_base(key):
    base = jax.random.normal(key, (CLIPS, TOKENS, HEADS * HEAD_DIM), jnp.float32)
    return jnp.clip(base, -5.0, 5.0)


def draw_video_key(key, part):
    keys_base = video_base(key)
    return keys_base.astype(jnp.bfloat16)


def draw_video_query(key, part):
    key = jax.random.fold_in(key, 7)
    queries = jnp.clip(jax.random.normal(key, (CLIPS, TOKENS, HEADS * HEAD_DIM), jnp.float32), -5.0, 5.0)
    return queries.astype(jnp.bfloat16)


def draw_prompt_length(key, part):
    key = jax.random.fold_in(key, 5)
    lengths = jax.random.randint(key, (CLIPS,), max(1, PROMPT // 8), PROMPT + 1)
    longest = jax.random.randint(jax.random.fold_in(key, 6), (), 0, CLIPS)
    return jnp.where(jnp.arange(CLIPS) == longest, PROMPT, lengths).astype(jnp.int32)


def block_scale(own_key, shape, cuts, smallest, high):
    level = 1.0
    for position, shards_of in cuts:
        draws = jax.random.uniform(jax.random.fold_in(jax.random.fold_in(own_key, 6), position), (shards_of,), jnp.float32, smallest / len(cuts), high / len(cuts))
        level = level * jnp.repeat(jnp.exp(draws), shape[position] // shards_of).reshape((-1,) + (1,) * (len(shape) - 1 - position))
    return level


def gaussian(own_key, extent, scale, reach, shards=(), dtype=jnp.bfloat16):
    gain = block_scale(own_key, extent, shards, -0.22, 0.18) if shards else 1.0
    result = jax.random.normal(own_key, extent, jnp.float32) * scale * gain
    return jnp.minimum(jnp.maximum(result, -reach), reach).astype(dtype)


def setup_inputs(seed: int = 0) -> dict:
    key_of = jax.random.split(jax.random.key(seed), 12)
    text_context = gaussian(key_of[0], (CLIPS, PROMPT, D_TEXT), 1.0, 6.0, ((0, 32), (2, 8)))
    text_residual = gaussian(key_of[1], (CLIPS, PROMPT, D_TEXT), 1.0, 6.0, ((0, 32),))
    text_out_weight = gaussian(key_of[2], (D_TEXT, D_TEXT), D_TEXT ** -0.5, 0.09375, ((0, 8),))
    text_gain = jnp.clip(1.0 + 0.18 * jax.random.normal(key_of[3], (D_TEXT,), jnp.float32), 0.1, 1.9)
    prompt_length = draw_prompt_length(jax.random.fold_in(key_of[11], 71), 0)
    key_weight = gaussian(key_of[5], (D_TEXT, HEADS * HEAD_DIM), D_TEXT ** -0.5, 0.09375, ((0, 32), (1, 8)))
    value_weight = gaussian(key_of[6], (D_TEXT, HEADS * HEAD_DIM), D_TEXT ** -0.5, 0.09375, ((0, 32), (1, 8)))
    video_query = draw_video_query(jax.random.fold_in(key_of[11], 71), 0)
    video_key = draw_video_key(jax.random.fold_in(key_of[11], 71), 0)
    video_value = gaussian(key_of[9], (CLIPS, TOKENS, HEADS * HEAD_DIM), 1.0, 6.0, ((0, 32), (1, 8)))
    out_cotangent = gaussian(key_of[10], (CLIPS, TOKENS, HEADS * HEAD_DIM), 1.0, 6.0, ((0, 32), (1, 8)))
    return {"text_context": text_context, "text_residual": text_residual, "text_out_weight": text_out_weight, "text_gain": text_gain, "prompt_length": prompt_length, "key_weight": key_weight, "value_weight": value_weight, "video_query": video_query, "video_key": video_key, "video_value": video_value, "out_cotangent": out_cotangent}


EPSILON = 1e-06

def attend_clip(item):
    queries, keys, values, cotangent, text_keys, text_values, length = item
    count = queries.shape[0]
    prompt = text_keys.shape[0]
    scale = 1.0 / math.sqrt(HEAD_DIM)
    query_heads = queries.reshape(count, HEADS, HEAD_DIM).astype(jnp.float32)
    grad_heads = cotangent.reshape(count, HEADS, HEAD_DIM).astype(jnp.float32)
    keys_all = jnp.concatenate([keys, text_keys], 0).reshape(count + prompt, HEADS, HEAD_DIM).astype(jnp.float32)
    values_all = jnp.concatenate([values, text_values], 0).reshape(count + prompt, HEADS, HEAD_DIM).astype(jnp.float32)
    allowed = jnp.arange(count + prompt) < count + length
    scores = jnp.einsum('qhd,khd->hqk', query_heads, keys_all) * scale
    scores = jnp.where(allowed[None, None, :], scores, -jnp.inf)
    peak = lax.optimization_barrier(jnp.max(scores, axis=2, keepdims=True))
    weights = jnp.exp(scores - peak)
    probs = weights / lax.optimization_barrier(jnp.sum(weights, axis=2, keepdims=True))
    probs_low = probs.astype(jnp.bfloat16).astype(jnp.float32)
    attended = jnp.einsum('hqk,khd->qhd', probs_low, values_all).astype(jnp.bfloat16)
    prob_grad = jnp.einsum('qhd,khd->hqk', grad_heads, values_all)
    center = lax.optimization_barrier(jnp.sum(probs * prob_grad, axis=2, keepdims=True))
    score_grad = (probs * (prob_grad - center) * scale).astype(jnp.bfloat16).astype(jnp.float32)
    query_grad = jnp.einsum('hqk,khd->qhd', score_grad, keys_all).astype(jnp.bfloat16)
    all_key_grad = jnp.einsum('hqk,qhd->khd', score_grad, query_heads).astype(jnp.bfloat16)
    all_value_grad = jnp.einsum('hqk,qhd->khd', probs_low, grad_heads).astype(jnp.bfloat16)
    width = HEADS * HEAD_DIM
    all_key_grad = all_key_grad.reshape(count + prompt, width)
    all_value_grad = all_value_grad.reshape(count + prompt, width)
    return (attended.reshape(count, width), query_grad.reshape(count, width), all_key_grad[:count], all_value_grad[:count], all_key_grad[count:], all_value_grad[count:])

def reference(text_context, text_residual, text_out_weight, text_gain, prompt_length, key_weight, value_weight, video_query, video_key, video_value, out_cotangent):
    flat_context = text_context.reshape(CLIPS * PROMPT, D_TEXT)
    summed = text_residual.reshape(CLIPS * PROMPT, D_TEXT).astype(jnp.float32) + jnp.dot(flat_context, text_out_weight, preferred_element_type=jnp.float32)
    mean_square = lax.optimization_barrier(jnp.mean(summed * summed, axis=1, keepdims=True))
    text = (summed * lax.rsqrt(mean_square + EPSILON) * text_gain).astype(jnp.bfloat16)
    text_keys = jnp.dot(text, key_weight, preferred_element_type=jnp.float32).astype(jnp.bfloat16)
    text_values = jnp.dot(text, value_weight, preferred_element_type=jnp.float32).astype(jnp.bfloat16)
    width = HEADS * HEAD_DIM
    text_keys = text_keys.reshape(CLIPS, PROMPT, width)
    text_values = text_values.reshape(CLIPS, PROMPT, width)
    results = lax.map(attend_clip, (video_query, video_key, video_value, out_cotangent, text_keys, text_values, prompt_length))
    attended, query_grad, key_grad, value_grad, text_key_grad, text_value_grad = results
    key_weight_grad = jnp.dot(text.T, text_key_grad.reshape(CLIPS * PROMPT, width), preferred_element_type=jnp.float32)
    value_weight_grad = jnp.dot(text.T, text_value_grad.reshape(CLIPS * PROMPT, width), preferred_element_type=jnp.float32)
    return (attended, query_grad, key_grad, value_grad, key_weight_grad, value_weight_grad)
```

```python
import math

import jax
import jax.numpy as jnp
from jax import lax
from jax.experimental import pallas as pl
from jax.experimental.pallas import tpu as pltpu
from jax.sharding import PartitionSpec as P

MESH = pl.DeviceIdType.MESH
BF = jnp.bfloat16
F32 = jnp.float32

HEAD_DIM = 128
EPSILON = 1e-06
SEQ = 8
ZS = 8
GROUP = 4
HEADS_HERE = 3
ROWS = 128
TOKENS = SEQ * ROWS
PROMPT = 128
ALL_ROWS = TOKENS + PROMPT
D_TEXT = 4096
SHARE = D_TEXT // SEQ
WIDTH = HEADS_HERE * HEAD_DIM
QUERY_BLOCK = 512
EXP2_SCALE = math.log2(math.e) / math.sqrt(HEAD_DIM)
SCALE = 1.0 / math.sqrt(HEAD_DIM)


def nn(left, right):
    return jnp.dot(left, right, preferred_element_type=F32)


def nt(left, right):
    return lax.dot_general(left, right, (((1,), (1,)), ((), ())), preferred_element_type=F32)


def tn(left, right):
    return lax.dot_general(left, right, (((0,), (0,)), ((), ())), preferred_element_type=F32)


def block128(index):
    return pl.ds(pl.multiple_of(index * 128, 128), 128)


def kernel(
    length_ref,
    context,
    gain,
    residual,
    out_weight,
    key_weight,
    value_weight,
    video_query,
    video_key,
    video_value,
    out_cotangent,
    attended,
    query_grad,
    key_grad,
    value_grad,
    key_weight_grad,
    value_weight_grad,
    q,
    k,
    v,
    do,
    out,
    dq,
    dk,
    dv,
    dk_total,
    dv_total,
    w_out,
    res,
    part,
    part_in,
    piece,
    square,
    gathered,
    squares,
    square_in,
    text,
    text_t,
    wk,
    wv,
    kv_part,
    kv_own,
    kv_in,
    dkv,
    dkv_all,
    grads,
    grads_in,
    in_s,
    in_r,
    out_s,
    out_r,
    w_s,
    w_r,
    rs_s,
    rs_r,
    load_sem,
    res_sem,
    ga_s,
    ga_r,
    gs_s,
    gs_r,
    ag_s,
    ag_r,
    as_s,
    as_r,
    kv_s,
    kv_r,
    dk_s,
    dk_r,
    wg_s,
    wg_r,
):
    dp = lax.axis_index("dp")
    seq = lax.axis_index("seq")
    y_lo = dp // 16
    z = (dp // 2) % 8
    core = dp % 2
    group = y_lo * 2 + core

    def seq_peer(d):
        return (dp, ((seq // 2 + d // 2) % 4) * 2 + (seq % 2 + d % 2) % 2)

    def group_index(i):
        return ((y_lo + i // 2) % 2) * 2 + (core + i % 2) % 2

    def group_peer(i):
        return (((y_lo + i // 2) % 2) * 16 + z * 2 + (core + i % 2) % 2, seq)

    def z_peer(i):
        return (y_lo * 16 + ((z + i) % 8) * 2 + core, seq)

    def remote(src, dst, send, recv, peer):
        return pltpu.make_async_remote_copy(
            src_ref=src, dst_ref=dst, send_sem=send, recv_sem=recv, device_id=peer, device_id_type=MESH
        )

    def loop(low, high, step):
        def run(i, carry):
            step(i)
            return carry

        lax.fori_loop(low, high, run, 0)


    def w_load(d, half):
        target = seq_peer(d)[1]
        columns = pl.ds(pl.multiple_of(half * 2048 + target * 256, 256), 256)
        return pltpu.make_async_copy(
            out_weight.at[:, columns], w_out.at[d, :, pl.ds(half * 256, 256)], load_sem.at[d, half]
        )

    def res_load(half):
        columns = pl.ds(pl.multiple_of(half * 2048 + seq * 256, 256), 256)
        return pltpu.make_async_copy(
            residual.at[:, columns], res.at[:, pl.ds(half * 256, 256)], res_sem.at[half]
        )

    def weight_copy(n, i):
        source, target = ((key_weight, wk), (value_weight, wv))[n]
        return remote(source, target.at[z], w_s.at[n, i], w_r.at[n, i], z_peer(i))

    def weight_own(n):
        source, target = ((key_weight, wk), (value_weight, wv))[n]
        return pltpu.make_async_copy(source, target.at[z], w_r.at[n, 0])

    sources = (video_query, video_key, video_value, out_cotangent)
    landings = (q, k, v, do)
    results = (out, dq, dk, dv)
    targets = (attended, query_grad, key_grad, value_grad)

    def in_copy(n, h, d):
        peer = seq_peer(d)
        return remote(
            sources[n].at[:, block128(peer[1] * HEADS_HERE + h)],
            landings[n].at[h, block128(seq)],
            in_s.at[n, h, d],
            in_r.at[n, h, d],
            peer,
        )

    def in_own(n, h):
        return pltpu.make_async_copy(
            sources[n].at[:, block128(seq * HEADS_HERE + h)],
            landings[n].at[h, block128(seq)],
            in_r.at[n, h, 0],
        )

    def out_copy(n, h, d):
        peer = seq_peer(d)
        return remote(
            results[n].at[h, block128(peer[1])],
            targets[n].at[:, block128(seq * HEADS_HERE + h)],
            out_s.at[n, h, d],
            out_r.at[n, h, d],
            peer,
        )

    def out_own(n, h):
        return pltpu.make_async_copy(
            results[n].at[h, block128(seq)],
            targets[n].at[:, block128(seq * HEADS_HERE + h)],
            out_r.at[n, h, 0],
        )

    def part_copy(d):
        return remote(part.at[d], part_in.at[d], rs_s.at[d], rs_r.at[d], seq_peer(d))

    def piece_copy(i):
        return remote(
            piece.at[group_index(i)], gathered.at[group], ga_s.at[i], ga_r.at[i], group_peer(i)
        )

    def square_copy(i):
        return remote(square, squares.at[group], gs_s.at[i], gs_r.at[i], group_peer(i))

    def text_copy(i, d):
        g = group_index(i)
        return remote(
            gathered.at[g], text.at[block128(g), block128(seq)], ag_s.at[i, d], ag_r.at[i, d], seq_peer(d)
        )

    def squares_copy(d):
        return remote(squares, square_in.at[d], as_s.at[d], as_r.at[d], seq_peer(d))

    def kv_copy(i):
        return remote(kv_part.at[i], kv_in.at[i], kv_s.at[i], kv_r.at[i], group_peer(i))

    def dkv_copy(h, i):
        return remote(dkv.at[h], dkv_all.at[h, group], dk_s.at[h, i], dk_r.at[h, i], group_peer(i))

    def grad_copy(h, i):
        return remote(grads.at[h, (z + i) % 8], grads_in.at[h, i], wg_s.at[h, i], wg_r.at[h, i], z_peer(i))

    def send_head_in(h):
        def step(d):
            for n in range(4):
                in_copy(n, h, d).start()

        loop(1, SEQ, step)


    barrier = pltpu.get_barrier_semaphore()

    def greet(peer):
        pl.semaphore_signal(barrier, inc=1, device_id=peer, device_id_type=MESH)

    loop(1, SEQ, lambda d: greet(seq_peer(d)))
    loop(1, GROUP, lambda i: greet(group_peer(i)))
    loop(1, ZS, lambda i: greet(z_peer(i)))

    def start_loads(i):
        d = (i + 1) % SEQ
        for half in range(2):
            w_load(d, half).start()

    loop(0, SEQ, start_loads)
    for half in range(2):
        res_load(half).start()
    for n in range(2):
        weight_own(n).start()
    for h in range(HEADS_HERE):
        for n in range(4):
            in_own(n, h).start()
    pl.semaphore_wait(barrier, SEQ - 1 + GROUP - 1 + ZS - 1)


    def project(d):
        for half in range(2):
            w_load(d, half).wait()
        return nn(context[...], w_out[d])

    def project_step(d):
        part[d] = project(d).astype(BF)
        part_copy(d).start()

    loop(1, SEQ, project_step)

    def weight_step(i):
        for n in range(2):
            weight_copy(n, i).start()

    loop(1, ZS, weight_step)
    send_head_in(0)

    for half in range(2):
        res_load(half).wait()
    summed = project(0) + res[...].astype(F32)
    for d in range(1, SEQ):
        part_copy(d).wait_recv()
        summed = summed + part_in[d].astype(F32)
    square[...] = lax.dot_general(
        jnp.ones((8, SHARE), F32),
        summed * summed,
        (((1,), (1,)), ((), ())),
        precision=lax.Precision.HIGHEST,
        preferred_element_type=F32,
    )
    for half in range(2):
        columns = pl.ds(pl.multiple_of(half * 2048 + seq * 256, 256), 256)
        scaled = (summed[:, half * 256 : (half + 1) * 256] * gain[:, columns]).astype(BF)
        for c in range(2):
            piece[half * 2 + c] = scaled[:, c * 128 : (c + 1) * 128]
    loop(1, GROUP, lambda i: piece_copy(i).start())
    loop(1, GROUP, lambda i: square_copy(i).start())
    gathered[group] = piece[group]
    squares[group] = square[...]


    def own_text():
        return pltpu.make_async_copy(
            gathered.at[group], text.at[block128(group), block128(seq)], ag_r.at[0, 0]
        )

    def other_text(i):
        g = group_index(i)
        return pltpu.make_async_copy(
            gathered.at[g], text.at[block128(g), block128(seq)], ag_r.at[i, 0]
        )

    own_text().start()
    loop(1, SEQ, lambda d: text_copy(0, d).start())

    def spread(i):
        piece_copy(i).wait_recv()
        other_text(i).start()
        loop(1, SEQ, lambda d: text_copy(i, d).start())

    loop(1, GROUP, spread)
    loop(1, GROUP, lambda i: square_copy(i).wait_recv())
    loop(1, SEQ, lambda d: squares_copy(d).start())
    square_in[0] = squares[...]

    send_head_in(1)
    send_head_in(2)

    def weight_wait(i):
        for n in range(2):
            weight_copy(n, i).wait_recv()

    loop(1, ZS, weight_wait)
    for n in range(2):
        weight_own(n).wait()
    loop(1, SEQ, lambda d: squares_copy(d).wait_recv())
    own_text().wait()
    loop(1, GROUP, lambda i: other_text(i).wait())

    def text_wait(d):
        loop(0, GROUP, lambda i: text_copy(i, d).wait_recv())

    loop(1, SEQ, text_wait)

    total = square_in[0]
    for d in range(1, SEQ):
        total = total + square_in[d]
    for g in range(GROUP):
        mean = jnp.transpose(jnp.broadcast_to(total[g, 0:1, :], (128, 128)))[:, 0:1] * (1.0 / D_TEXT)
        rows = pl.ds(g * 128, 128)
        text[rows, :] = (text[rows, :].astype(F32) * lax.rsqrt(mean + EPSILON)).astype(BF)


    def project_kv(g):
        rows = text[block128(g), :]
        return (
            nn(rows, wk[...].reshape(ZS * 128, WIDTH)),
            nn(rows, wv[...].reshape(ZS * 128, WIDTH)),
        )

    def kv_step(i):
        keys, values = project_kv(group_index(i))
        kv_part[i, :, :WIDTH] = keys.astype(BF)
        kv_part[i, :, WIDTH:] = values.astype(BF)
        kv_copy(i).start()

    loop(1, GROUP, kv_step)
    keys, values = project_kv(group)
    kv_own[:, :WIDTH] = keys
    kv_own[:, WIDTH:] = values
    for g in range(GROUP):
        text_t[:, g * 128 : (g + 1) * 128] = jnp.transpose(text[g * 128 : (g + 1) * 128, :])
    for i in range(1, GROUP):
        kv_copy(i).wait_recv()
        kv_own[...] += kv_in[i].astype(F32)
    for h in range(HEADS_HERE):
        k[h, TOKENS:, :] = kv_own[:, h * 128 : (h + 1) * 128].astype(BF)
        v[h, TOKENS:, :] = kv_own[:, WIDTH + h * 128 : WIDTH + (h + 1) * 128].astype(BF)


    length = length_ref[0]

    def attend(h, i):
        rows = pl.ds(pl.multiple_of(i * QUERY_BLOCK, QUERY_BLOCK), QUERY_BLOCK)
        queries, cotangent, keys, values = q[h, rows, :], do[h, rows, :], k[h], v[h]
        scores = nt(queries, keys)
        allowed = lax.broadcasted_iota(jnp.int32, (1, PROMPT), 1) < length
        scores = jnp.concatenate(
            [scores[:, :TOKENS], jnp.where(allowed, scores[:, TOKENS:], -jnp.inf)], axis=1
        )
        peak = jnp.max(scores, axis=1, keepdims=True)
        weights = jnp.exp2((scores - peak) * EXP2_SCALE)
        weights_low = weights.astype(BF)
        sums = nn(weights_low, jnp.concatenate([values, jnp.ones_like(values)], axis=1))
        inverse = 1.0 / sums[:, HEAD_DIM:]
        output = sums[:, :HEAD_DIM] * inverse
        out[h, rows, :] = output.astype(BF)
        cotangent_wide = cotangent.astype(F32)
        center = jnp.sum(cotangent_wide * output, axis=1, keepdims=True)
        score_grad = (weights * (nt(cotangent, values) - center)).astype(BF)
        scaled = inverse * SCALE
        dq[h, rows, :] = (nn(score_grad, keys) * scaled).astype(BF)
        dk_total[...] += tn(score_grad, (queries.astype(F32) * scaled).astype(BF))
        dv_total[...] += tn(weights_low, (cotangent_wide * inverse).astype(BF))

    def weight_grads(h):
        loop(1, GROUP, lambda i: dkv_copy(h, i).wait_recv())
        products = nn(text_t[...], dkv_all[h].reshape(GROUP * 128, 256))
        grads[h] = products.astype(BF).reshape(ZS, 128, 256)
        loop(1, ZS, lambda i: grad_copy(h, i).start())

    def head(h):
        def arrived(d):
            for n in range(4):
                in_copy(n, h, d).wait_recv()

        loop(1, SEQ, arrived)
        for n in range(4):
            in_own(n, h).wait()
        dk_total[...] = jnp.zeros_like(dk_total)
        dv_total[...] = jnp.zeros_like(dv_total)
        loop(0, TOKENS // QUERY_BLOCK, lambda i: attend(h, i))
        dk[h] = dk_total[:TOKENS, :].astype(BF)
        dv[h] = dv_total[:TOKENS, :].astype(BF)
        both = jnp.concatenate([dk_total[TOKENS:, :], dv_total[TOKENS:, :]], axis=1).astype(BF)
        dkv[h] = both
        dkv_all[h, group] = both
        loop(1, GROUP, lambda i: dkv_copy(h, i).start())

        def leave(d):
            for n in range(4):
                out_copy(n, h, d).start()

        loop(1, SEQ, leave)
        for n in range(4):
            out_own(n, h).start()

        @pl.when(h > 0)
        def _():
            weight_grads(h - 1)

    loop(0, HEADS_HERE, head)
    weight_grads(HEADS_HERE - 1)
    for h in range(HEADS_HERE):
        total = grads[h, z].astype(F32)
        for i in range(1, ZS):
            grad_copy(h, i).wait_recv()
            total = total + grads_in[h, i].astype(F32)
        key_weight_grad[:, h * 128 : (h + 1) * 128] = total[:, :128]
        value_weight_grad[:, h * 128 : (h + 1) * 128] = total[:, 128:]


    def finish(h):
        def each(d):
            for n in range(4):
                out_copy(n, h, d).wait_recv()
                out_copy(n, h, d).wait_send()
                in_copy(n, h, d).wait_send()

        loop(1, SEQ, each)
        for n in range(4):
            out_own(n, h).wait()
        loop(1, GROUP, lambda i: dkv_copy(h, i).wait_send())
        loop(1, ZS, lambda i: grad_copy(h, i).wait_send())

    loop(0, HEADS_HERE, finish)

    def finish_seq(d):
        part_copy(d).wait_send()
        squares_copy(d).wait_send()
        loop(0, GROUP, lambda i: text_copy(i, d).wait_send())

    loop(1, SEQ, finish_seq)

    def finish_group(i):
        piece_copy(i).wait_send()
        square_copy(i).wait_send()
        kv_copy(i).wait_send()

    loop(1, GROUP, finish_group)

    def finish_z(i):
        for n in range(2):
            weight_copy(n, i).wait_send()

    loop(1, ZS, finish_z)


def body(
    text_context,
    text_residual,
    text_out_weight,
    text_gain,
    prompt_length,
    key_weight,
    value_weight,
    video_query,
    video_key,
    video_value,
    out_cotangent,
):
    vmem = pl.BlockSpec(memory_space=pltpu.VMEM)
    hbm = pl.BlockSpec(memory_space=pl.ANY)
    smem = pl.BlockSpec(memory_space=pltpu.SMEM)
    dma = pltpu.SemaphoreType.DMA
    tokens = jax.ShapeDtypeStruct((ROWS, SEQ * WIDTH), BF)
    weights = jax.ShapeDtypeStruct((128, WIDTH), F32)
    scratch = [
        pltpu.VMEM((HEADS_HERE, TOKENS, HEAD_DIM), BF),
        pltpu.VMEM((HEADS_HERE, ALL_ROWS, HEAD_DIM), BF),
        pltpu.VMEM((HEADS_HERE, ALL_ROWS, HEAD_DIM), BF),
        pltpu.VMEM((HEADS_HERE, TOKENS, HEAD_DIM), BF),
        pltpu.VMEM((HEADS_HERE, TOKENS, HEAD_DIM), BF),
        pltpu.VMEM((HEADS_HERE, TOKENS, HEAD_DIM), BF),
        pltpu.VMEM((HEADS_HERE, TOKENS, HEAD_DIM), BF),
        pltpu.VMEM((HEADS_HERE, TOKENS, HEAD_DIM), BF),
        pltpu.VMEM((ALL_ROWS, HEAD_DIM), F32),
        pltpu.VMEM((ALL_ROWS, HEAD_DIM), F32),
        pltpu.VMEM((SEQ, SHARE, SHARE), BF),
        pltpu.VMEM((PROMPT, SHARE), BF),
        pltpu.VMEM((SEQ, PROMPT, SHARE), BF),
        pltpu.VMEM((SEQ, PROMPT, SHARE), BF),
        pltpu.VMEM((GROUP, PROMPT, 128), BF),
        pltpu.VMEM((8, PROMPT), F32),
        pltpu.VMEM((GROUP, PROMPT, 128), BF),
        pltpu.VMEM((GROUP, 8, PROMPT), F32),
        pltpu.VMEM((SEQ, GROUP, 8, PROMPT), F32),
        pltpu.VMEM((GROUP * PROMPT, SEQ * 128), BF),
        pltpu.VMEM((SEQ * 128, GROUP * PROMPT), BF),
        pltpu.VMEM((ZS, 128, WIDTH), BF),
        pltpu.VMEM((ZS, 128, WIDTH), BF),
        pltpu.VMEM((GROUP, PROMPT, 2 * WIDTH), BF),
        pltpu.VMEM((PROMPT, 2 * WIDTH), F32),
        pltpu.VMEM((GROUP, PROMPT, 2 * WIDTH), BF),
        pltpu.VMEM((HEADS_HERE, PROMPT, 256), BF),
        pltpu.VMEM((HEADS_HERE, GROUP, PROMPT, 256), BF),
        pltpu.VMEM((HEADS_HERE, ZS, 128, 256), BF),
        pltpu.VMEM((HEADS_HERE, ZS, 128, 256), BF),
        dma((4, HEADS_HERE, SEQ)),
        dma((4, HEADS_HERE, SEQ)),
        dma((4, HEADS_HERE, SEQ)),
        dma((4, HEADS_HERE, SEQ)),
        dma((2, ZS)),
        dma((2, ZS)),
        dma((SEQ,)),
        dma((SEQ,)),
        dma((SEQ, 2)),
        dma((2,)),
        dma((GROUP,)),
        dma((GROUP,)),
        dma((GROUP,)),
        dma((GROUP,)),
        dma((GROUP, SEQ)),
        dma((GROUP, SEQ)),
        dma((SEQ,)),
        dma((SEQ,)),
        dma((GROUP,)),
        dma((GROUP,)),
        dma((HEADS_HERE, GROUP)),
        dma((HEADS_HERE, GROUP)),
        dma((HEADS_HERE, ZS)),
        dma((HEADS_HERE, ZS)),
    ]
    attended, query_grad, key_grad, value_grad, key_weight_grad, value_weight_grad = pl.pallas_call(
        kernel,
        out_shape=[tokens] * 4 + [weights] * 2,
        in_specs=[smem, vmem, vmem] + [hbm] * 8,
        out_specs=[hbm] * 4 + [vmem] * 2,
        scratch_shapes=scratch,
        name="joint_attention",
        compiler_params=pltpu.CompilerParams(
            collective_id=0, has_side_effects=True, vmem_limit_bytes=56 * 1024 * 1024
        ),
    )(
        prompt_length,
        text_context[0],
        text_gain.reshape(1, D_TEXT),
        text_residual[0],
        text_out_weight,
        key_weight,
        value_weight,
        video_query[0],
        video_key[0],
        video_value[0],
        out_cotangent[0],
    )
    return (
        attended[None],
        query_grad[None],
        key_grad[None],
        value_grad[None],
        key_weight_grad,
        value_weight_grad,
    )


def solution(mesh):
    in_specs = (
        P("dp", None, "seq"),
        P("dp", None, None),
        P("seq", None),
        P(),
        P("dp"),
        P("dp", "seq"),
        P("dp", "seq"),
        P("dp", "seq", None),
        P("dp", "seq", None),
        P("dp", "seq", None),
        P("dp", "seq", None),
    )
    out_specs = (
        P("dp", "seq", None),
        P("dp", "seq", None),
        P("dp", "seq", None),
        P("dp", "seq", None),
        P("dp", "seq"),
        P("dp", "seq"),
    )
    return jax.shard_map(body, mesh=mesh, in_specs=in_specs, out_specs=out_specs, check_vma=False)
```

```python
import math

import jax
import jax.numpy as jnp
from jax import lax
from jax.experimental import pallas as pl
from jax.experimental.pallas import tpu as pltpu
from jax.sharding import PartitionSpec as P

MESH = pl.DeviceIdType.MESH
BF = jnp.bfloat16
F32 = jnp.float32

HEAD_DIM = 128
EPSILON = 1e-06
SEQ = 8
ZS = 8
GROUP = 4
HEADS_HERE = 3
ROWS = 128
TOKENS = SEQ * ROWS
PROMPT = 128
ALL_ROWS = TOKENS + PROMPT
D_TEXT = 4096
SHARE = D_TEXT // SEQ
WIDTH = HEADS_HERE * HEAD_DIM
QUERY_BLOCK = 512
EXP2_SCALE = math.log2(math.e) / math.sqrt(HEAD_DIM)
SCALE = 1.0 / math.sqrt(HEAD_DIM)


def nn(left, right):
    return jnp.dot(left, right, preferred_element_type=F32)


def nt(left, right):
    return lax.dot_general(left, right, (((1,), (1,)), ((), ())), preferred_element_type=F32)


def tn(left, right):
    return lax.dot_general(left, right, (((0,), (0,)), ((), ())), preferred_element_type=F32)


def block128(index):
    return pl.ds(pl.multiple_of(index * 128, 128), 128)


def kernel(
    length_ref,
    context,
    gain,
    residual,
    out_weight,
    key_weight,
    value_weight,
    video_query,
    video_key,
    video_value,
    out_cotangent,
    attended,
    query_grad,
    key_grad,
    value_grad,
    key_weight_grad,
    value_weight_grad,
    q,
    k,
    v,
    do,
    out,
    dq,
    dk,
    dv,
    dk_total,
    dv_total,
    w_out,
    res,
    summed,
    part,
    part_in,
    piece,
    landed,
    text,
    text_t,
    wkv,
    kv_own,
    kv_core,
    kv_core_in,
    kv_far,
    kv_far_in,
    dkv_all,
    grads,
    grads_in,
    in_s,
    in_r,
    out_s,
    out_r,
    w_s,
    w_r,
    rs_s,
    rs_r,
    load_sem,
    res_sem,
    ag_s,
    ag_r,
    kc_s,
    kc_r,
    kf_s,
    kf_r,
    dk_s,
    dk_r,
    wg_s,
    wg_r,
):
    dp = lax.axis_index("dp")
    seq = lax.axis_index("seq")
    y_lo = dp // 16
    z = (dp // 2) % 8
    core = dp % 2

    def seq_of(d):
        return ((seq // 2 + d // 2) % 4) * 2 + (seq % 2 + d % 2) % 2

    def seq_peer(d):
        return (dp, seq_of(d))

    def group_peer(i, d):
        return (((y_lo + i // 2) % 2) * 16 + z * 2 + (core + i % 2) % 2, seq_of(d))

    def core_peer():
        return (dp + 1 - 2 * core, seq)

    def far_peer():
        return ((1 - y_lo) * 16 + z * 2 + core, seq)

    def z_peer(i):
        return (y_lo * 16 + ((z + i) % 8) * 2 + core, seq)

    def remote(src, dst, send, recv, peer):
        return pltpu.make_async_remote_copy(
            src_ref=src, dst_ref=dst, send_sem=send, recv_sem=recv, device_id=peer, device_id_type=MESH
        )

    def loop(low, high, step):
        def run(i, carry):
            step(i)
            return carry

        lax.fori_loop(low, high, run, 0)


    def w_load(d, half):
        columns = pl.ds(pl.multiple_of(half * 2048 + seq_of(d) * 256, 256), 256)
        return pltpu.make_async_copy(
            out_weight.at[:, columns], w_out.at[d, :, pl.ds(half * 256, 256)], load_sem.at[d, half]
        )

    def res_load(half):
        columns = pl.ds(pl.multiple_of(half * 2048 + seq * 256, 256), 256)
        return pltpu.make_async_copy(
            residual.at[:, columns], res.at[:, pl.ds(half * 256, 256)], res_sem.at[half]
        )

    def weight_copy(n, h, i):
        return remote(
            (key_weight, value_weight)[n].at[:, block128(h)],
            wkv.at[h, z, :, pl.ds(n * 128, 128)],
            w_s.at[n, h, i],
            w_r.at[n, h, i],
            z_peer(i),
        )

    def weight_own(n, h):
        return pltpu.make_async_copy(
            (key_weight, value_weight)[n].at[:, block128(h)],
            wkv.at[h, z, :, pl.ds(n * 128, 128)],
            w_r.at[n, h, 0],
        )

    sources = (video_query, video_key, video_value, out_cotangent)
    landings = (q, k, v, do)
    results = (out, dq, dk, dv)
    targets = (attended, query_grad, key_grad, value_grad)

    def in_copy(n, h, d):
        peer = seq_peer(d)
        return remote(
            sources[n].at[:, block128(peer[1] * HEADS_HERE + h)],
            landings[n].at[h, block128(seq)],
            in_s.at[n, h, d],
            in_r.at[n, h, d],
            peer,
        )

    def in_own(n, h):
        return pltpu.make_async_copy(
            sources[n].at[:, block128(seq * HEADS_HERE + h)],
            landings[n].at[h, block128(seq)],
            in_r.at[n, h, 0],
        )

    def out_copy(n, h, d):
        peer = seq_peer(d)
        return remote(
            results[n].at[h, block128(peer[1])],
            targets[n].at[:, block128(seq * HEADS_HERE + h)],
            out_s.at[n, h, d],
            out_r.at[n, h, d],
            peer,
        )

    def out_own(n, h):
        return pltpu.make_async_copy(
            results[n].at[h, block128(seq)],
            targets[n].at[:, block128(seq * HEADS_HERE + h)],
            out_r.at[n, h, 0],
        )

    def part_copy(d):
        return remote(part.at[d], part_in.at[d], rs_s.at[d], rs_r.at[d], seq_peer(d))

    def piece_copy(i, d):
        target = ((y_lo + i // 2) % 2) * 2 + (core + i % 2) % 2
        return remote(
            piece.at[target],
            landed.at[seq, (i % 2) * 2 + y_lo],
            ag_s.at[i, d],
            ag_r.at[i, d],
            group_peer(i, d),
        )

    def kv_core_copy(h):
        return remote(kv_core.at[h], kv_core_in.at[h], kc_s.at[h], kc_r.at[h], core_peer())

    def kv_far_copy(h):
        return remote(kv_far.at[h], kv_far_in.at[h], kf_s.at[h], kf_r.at[h], far_peer())

    def dkv_far(h):
        mine = dkv_all.at[h, y_lo]
        return remote(mine, mine, dk_s.at[h, 0], dk_r.at[h, 0], far_peer())

    def dkv_core(h, other):
        side = (1 - y_lo) if other else y_lo
        return remote(
            dkv_all.at[h, side],
            dkv_all.at[h, 2 + side],
            dk_s.at[h, 1 + other],
            dk_r.at[h, 1 + other],
            core_peer(),
        )

    def grad_copy(h, i):
        return remote(grads.at[h, (z + i) % 8], grads_in.at[h, i], wg_s.at[h, i], wg_r.at[h, i], z_peer(i))

    def send_head_in(h):
        for n in range(4):
            loop(1, SEQ, lambda d: in_copy(n, h, d).start())

    def all_group(step):
        loop(1, SEQ, lambda d: step(0, d))
        loop(1, GROUP, lambda i: loop(0, SEQ, lambda d: step(i, d)))


    barrier = pltpu.get_barrier_semaphore()

    def greet(peer):
        pl.semaphore_signal(barrier, inc=1, device_id=peer, device_id_type=MESH)

    all_group(lambda i, d: greet(group_peer(i, d)))
    loop(1, ZS, lambda i: greet(z_peer(i)))

    def start_loads(d):
        for half in range(2):
            w_load(d, half).start()

    loop(0, SEQ, start_loads)
    for half in range(2):
        res_load(half).start()
    for h in range(HEADS_HERE):
        for n in range(2):
            weight_own(n, h).start()
        for n in range(4):
            in_own(n, h).start()


    def project(d):
        for half in range(2):
            w_load(d, half).wait()
        return nn(context[...], w_out[d])

    for half in range(2):
        res_load(half).wait()
    summed[...] = project(0) + res[...].astype(F32)

    def project_step(d):
        part[d] = project(d).astype(BF)

    loop(1, SEQ, project_step)
    pl.semaphore_wait(barrier, GROUP * SEQ - 1 + ZS - 1)
    loop(1, SEQ, lambda d: part_copy(d).start())

    def send_weights(h):
        for n in range(2):
            loop(1, ZS, lambda i: weight_copy(n, h, i).start())

    send_weights(0)
    send_head_in(0)
    send_weights(1)
    send_weights(2)

    for d in range(1, SEQ):
        part_copy(d).wait_recv()
        summed[...] += part_in[d].astype(F32)
    total = summed[...]
    square = lax.dot_general(
        jnp.ones((16, SHARE), F32),
        total * total,
        (((1,), (1,)), ((), ())),
        precision=lax.Precision.HIGHEST,
        preferred_element_type=F32,
    )
    high = square.astype(BF).astype(F32)
    middle = (square - high).astype(BF).astype(F32)
    low = square - high - middle
    row = lax.broadcasted_iota(jnp.int32, (16, PROMPT), 0)
    square_rows = jnp.where(
        row == 0, high, jnp.where(row == 1, middle, jnp.where(row == 2, low, 0.0))
    ).astype(BF)
    for half in range(2):
        columns = pl.ds(pl.multiple_of(half * 2048 + seq * 256, 256), 256)
        scaled = (total[:, half * 256 : (half + 1) * 256] * gain[:, columns]).astype(BF)
        for c in range(2):
            piece[half * 2 + c, :PROMPT, :] = scaled[:, c * 128 : (c + 1) * 128]
            piece[half * 2 + c, PROMPT:, :] = square_rows
    all_group(lambda i, d: piece_copy(i, d).start())
    landed[seq, y_lo] = piece[y_lo * 2 + core]
    send_head_in(1)
    send_head_in(2)


    all_group(lambda i, d: piece_copy(i, d).wait_recv())
    for g in range(GROUP):
        rows = landed[0, g, PROMPT:, :].astype(F32)
        for s in range(1, SEQ):
            rows = rows + landed[s, g, PROMPT:, :].astype(F32)
        mean = jnp.sum(rows, axis=0, keepdims=True) * (1.0 / D_TEXT)
        inverse = lax.rsqrt(jnp.transpose(jnp.broadcast_to(mean, (128, 128))) + EPSILON)
        for s in range(SEQ):
            text[g * 128 : (g + 1) * 128, s * 128 : (s + 1) * 128] = (
                landed[s, g, :PROMPT, :].astype(F32) * inverse
            ).astype(BF)


    def project_kv(h):
        def arrived(i):
            for n in range(2):
                weight_copy(n, h, i).wait_recv()

        loop(1, ZS, arrived)
        for n in range(2):
            weight_own(n, h).wait()
        weights = wkv[h].reshape(ZS * 128, 256)
        kv_core[h] = nn(text[256:, :], weights).astype(BF)
        kv_core_copy(h).start()
        kv_own[h] = nn(text[:256, :], weights)

    def add_core(h):
        kv_core_copy(h).wait_recv()
        kv_own[h] += kv_core_in[h].astype(F32)
        kv_far[h] = kv_own[h, block128(1 - y_lo), :].astype(BF)
        kv_far_copy(h).start()

    loop(0, HEADS_HERE, project_kv)
    loop(0, HEADS_HERE, add_core)
    for g in range(GROUP):
        text_t[:, g * 128 : (g + 1) * 128] = jnp.transpose(text[g * 128 : (g + 1) * 128, :])


    length = length_ref[0]

    def attend(h, i):
        rows = pl.ds(pl.multiple_of(i * QUERY_BLOCK, QUERY_BLOCK), QUERY_BLOCK)
        queries, cotangent, keys, values = q[h, rows, :], do[h, rows, :], k[h], v[h]
        scores = nt(queries, keys)
        allowed = lax.broadcasted_iota(jnp.int32, (1, PROMPT), 1) < length
        scores = jnp.concatenate(
            [scores[:, :TOKENS], jnp.where(allowed, scores[:, TOKENS:], -jnp.inf)], axis=1
        )
        peak = jnp.max(scores, axis=1, keepdims=True)
        weights = jnp.exp2((scores - peak) * EXP2_SCALE)
        weights_low = weights.astype(BF)
        sums = nn(weights_low, jnp.concatenate([values, jnp.ones_like(values)], axis=1))
        inverse = 1.0 / sums[:, HEAD_DIM:]
        output = sums[:, :HEAD_DIM] * inverse
        out[h, rows, :] = output.astype(BF)
        cotangent_wide = cotangent.astype(F32)
        center = jnp.sum(cotangent_wide * output, axis=1, keepdims=True)
        score_grad = (weights * (nt(cotangent, values) - center)).astype(BF)
        scaled = inverse * SCALE
        dq[h, rows, :] = (nn(score_grad, keys) * scaled).astype(BF)
        dk_total[...] += tn(score_grad, (queries.astype(F32) * scaled).astype(BF))
        dv_total[...] += tn(weights_low, (cotangent_wide * inverse).astype(BF))

    def weight_grads(h):
        dkv_far(h).wait_recv()
        dkv_core(h, 1).start()
        dkv_core(h, 0).wait_recv()
        dkv_core(h, 1).wait_recv()
        products = nn(text_t[...], dkv_all[h].reshape(GROUP * 128, 256))
        grads[h] = products.astype(BF).reshape(ZS, 128, 256)
        loop(1, ZS, lambda i: grad_copy(h, i).start())

    def head(h):
        kv_far_copy(h).wait_recv()
        kv = kv_own[h, block128(y_lo), :] + kv_far_in[h].astype(F32)
        k[h, TOKENS:, :] = kv[:, :128].astype(BF)
        v[h, TOKENS:, :] = kv[:, 128:].astype(BF)
        for n in range(4):
            loop(1, SEQ, lambda d: in_copy(n, h, d).wait_recv())
            in_own(n, h).wait()
        dk_total[...] = jnp.zeros_like(dk_total)
        dv_total[...] = jnp.zeros_like(dv_total)
        loop(0, TOKENS // QUERY_BLOCK, lambda i: attend(h, i))
        dk[h] = dk_total[:TOKENS, :].astype(BF)
        dv[h] = dv_total[:TOKENS, :].astype(BF)
        dkv_all[h, y_lo] = jnp.concatenate(
            [dk_total[TOKENS:, :], dv_total[TOKENS:, :]], axis=1
        ).astype(BF)
        dkv_far(h).start()
        dkv_core(h, 0).start()
        for n in range(4):
            loop(1, SEQ, lambda d: out_copy(n, h, d).start())
            out_own(n, h).start()

        @pl.when(h > 0)
        def _():
            weight_grads(h - 1)

    loop(0, HEADS_HERE, head)
    weight_grads(HEADS_HERE - 1)
    for h in range(HEADS_HERE):
        total = grads[h, z].astype(F32)
        for i in range(1, ZS):
            grad_copy(h, i).wait_recv()
            total = total + grads_in[h, i].astype(F32)
        key_weight_grad[:, h * 128 : (h + 1) * 128] = total[:, :128]
        value_weight_grad[:, h * 128 : (h + 1) * 128] = total[:, 128:]


    def finish(h):
        for n in range(4):

            def each(d):
                out_copy(n, h, d).wait_recv()
                out_copy(n, h, d).wait_send()
                in_copy(n, h, d).wait_send()

            loop(1, SEQ, each)
            out_own(n, h).wait()
        kv_core_copy(h).wait_send()
        kv_far_copy(h).wait_send()
        dkv_far(h).wait_send()
        dkv_core(h, 0).wait_send()
        dkv_core(h, 1).wait_send()

        def finish_z(i):
            grad_copy(h, i).wait_send()
            for n in range(2):
                weight_copy(n, h, i).wait_send()

        loop(1, ZS, finish_z)

    loop(0, HEADS_HERE, finish)
    loop(1, SEQ, lambda d: part_copy(d).wait_send())
    all_group(lambda i, d: piece_copy(i, d).wait_send())


def hand_over(*refs):
    count = 6
    sources, targets, holds = refs[:count], refs[count : 2 * count], refs[2 * count : 3 * count]
    sem = refs[3 * count]
    parts = [(n, part) for part in range(2) for n in range(count)]

    def load(n, part):
        rows = pl.ds(part * 64, 64)
        return pltpu.make_async_copy(sources[n].at[rows], holds[n].at[rows], sem.at[0, n, part])

    def store(n, part):
        rows = pl.ds(part * 64, 64)
        return pltpu.make_async_copy(holds[n].at[rows], targets[n].at[rows], sem.at[1, n, part])

    for n, part in parts:
        load(n, part).start()
    for n, part in parts:
        load(n, part).wait()
        store(n, part).start()
    for n, part in parts:
        store(n, part).wait()


def body(
    text_context,
    text_residual,
    text_out_weight,
    text_gain,
    prompt_length,
    key_weight,
    value_weight,
    video_query,
    video_key,
    video_value,
    out_cotangent,
):
    vmem = pl.BlockSpec(memory_space=pltpu.VMEM)
    hbm = pl.BlockSpec(memory_space=pl.ANY)
    smem = pl.BlockSpec(memory_space=pltpu.SMEM)
    dma = pltpu.SemaphoreType.DMA
    tokens = jax.ShapeDtypeStruct((ROWS, SEQ * WIDTH), BF)
    weights = jax.ShapeDtypeStruct((128, WIDTH), F32)
    scratch = [
        pltpu.VMEM((HEADS_HERE, TOKENS, HEAD_DIM), BF),
        pltpu.VMEM((HEADS_HERE, ALL_ROWS, HEAD_DIM), BF),
        pltpu.VMEM((HEADS_HERE, ALL_ROWS, HEAD_DIM), BF),
        pltpu.VMEM((HEADS_HERE, TOKENS, HEAD_DIM), BF),
        pltpu.VMEM((HEADS_HERE, TOKENS, HEAD_DIM), BF),
        pltpu.VMEM((HEADS_HERE, TOKENS, HEAD_DIM), BF),
        pltpu.VMEM((HEADS_HERE, TOKENS, HEAD_DIM), BF),
        pltpu.VMEM((HEADS_HERE, TOKENS, HEAD_DIM), BF),
        pltpu.VMEM((ALL_ROWS, HEAD_DIM), F32),
        pltpu.VMEM((ALL_ROWS, HEAD_DIM), F32),
        pltpu.VMEM((SEQ, SHARE, SHARE), BF),
        pltpu.VMEM((PROMPT, SHARE), BF),
        pltpu.VMEM((PROMPT, SHARE), F32),
        pltpu.VMEM((SEQ, PROMPT, SHARE), BF),
        pltpu.VMEM((SEQ, PROMPT, SHARE), BF),
        pltpu.VMEM((GROUP, PROMPT + 16, 128), BF),
        pltpu.VMEM((SEQ, GROUP, PROMPT + 16, 128), BF),
        pltpu.VMEM((GROUP * PROMPT, SEQ * 128), BF),
        pltpu.VMEM((SEQ * 128, GROUP * PROMPT), BF),
        pltpu.VMEM((HEADS_HERE, ZS, 128, 256), BF),
        pltpu.VMEM((HEADS_HERE, 2 * PROMPT, 256), F32),
        pltpu.VMEM((HEADS_HERE, 2 * PROMPT, 256), BF),
        pltpu.VMEM((HEADS_HERE, 2 * PROMPT, 256), BF),
        pltpu.VMEM((HEADS_HERE, PROMPT, 256), BF),
        pltpu.VMEM((HEADS_HERE, PROMPT, 256), BF),
        pltpu.VMEM((HEADS_HERE, GROUP, PROMPT, 256), BF),
        pltpu.VMEM((HEADS_HERE, ZS, 128, 256), BF),
        pltpu.VMEM((HEADS_HERE, ZS, 128, 256), BF),
        dma((4, HEADS_HERE, SEQ)),
        dma((4, HEADS_HERE, SEQ)),
        dma((4, HEADS_HERE, SEQ)),
        dma((4, HEADS_HERE, SEQ)),
        dma((2, HEADS_HERE, ZS)),
        dma((2, HEADS_HERE, ZS)),
        dma((SEQ,)),
        dma((SEQ,)),
        dma((SEQ, 2)),
        dma((2,)),
        dma((GROUP, SEQ)),
        dma((GROUP, SEQ)),
        dma((HEADS_HERE,)),
        dma((HEADS_HERE,)),
        dma((HEADS_HERE,)),
        dma((HEADS_HERE,)),
        dma((HEADS_HERE, 3)),
        dma((HEADS_HERE, 3)),
        dma((HEADS_HERE, ZS)),
        dma((HEADS_HERE, ZS)),
    ]
    shapes = [tokens] * 4 + [weights] * 2
    made = pl.pallas_call(
        kernel,
        out_shape=shapes,
        in_specs=[smem, vmem, vmem] + [hbm] * 8,
        out_specs=[hbm] * 4 + [vmem] * 2,
        scratch_shapes=scratch,
        name="joint_attention",
        compiler_params=pltpu.CompilerParams(
            collective_id=0, has_side_effects=True, vmem_limit_bytes=56 * 1024 * 1024
        ),
    )(
        prompt_length,
        text_context[0],
        text_gain.reshape(1, D_TEXT),
        text_residual[0],
        text_out_weight,
        key_weight,
        value_weight,
        video_query[0],
        video_key[0],
        video_value[0],
        out_cotangent[0],
    )
    attended, query_grad, key_grad, value_grad, key_weight_grad, value_weight_grad = pl.pallas_call(
        hand_over,
        out_shape=shapes,
        in_specs=[hbm] * 6,
        out_specs=[hbm] * 6,
        scratch_shapes=[pltpu.VMEM(x.shape, x.dtype) for x in shapes] + [dma((2, 6, 2))],
        name="hand_over",
    )(*made)
    return (
        attended[None],
        query_grad[None],
        key_grad[None],
        value_grad[None],
        key_weight_grad,
        value_weight_grad,
    )


def solution(mesh):
    in_specs = (
        P("dp", None, "seq"),
        P("dp", None, None),
        P("seq", None),
        P(),
        P("dp"),
        P("dp", "seq"),
        P("dp", "seq"),
        P("dp", "seq", None),
        P("dp", "seq", None),
        P("dp", "seq", None),
        P("dp", "seq", None),
    )
    out_specs = (
        P("dp", "seq", None),
        P("dp", "seq", None),
        P("dp", "seq", None),
        P("dp", "seq", None),
        P("dp", "seq"),
        P("dp", "seq"),
    )
    return jax.shard_map(body, mesh=mesh, in_specs=in_specs, out_specs=out_specs, check_vma=False)
```

```python
import math

import jax
import jax.numpy as jnp
from jax import lax
from jax.experimental import pallas as pl
from jax.experimental.pallas import tpu as pltpu
from jax.sharding import PartitionSpec as P

MESH = pl.DeviceIdType.MESH
BF = jnp.bfloat16
F32 = jnp.float32

HEAD_DIM = 128
EPSILON = 1e-06
SEQ = 8
ZS = 8
GROUP = 4
HEADS_HERE = 3
ROWS = 128
TOKENS = SEQ * ROWS
PROMPT = 128
ALL_ROWS = TOKENS + PROMPT
D_TEXT = 4096
SHARE = D_TEXT // SEQ
WIDTH = HEADS_HERE * HEAD_DIM
QUERY_BLOCK = 512
EXP2_SCALE = math.log2(math.e) / math.sqrt(HEAD_DIM)
SCALE = 1.0 / math.sqrt(HEAD_DIM)


def nn(left, right):
    return jnp.dot(left, right, preferred_element_type=F32)


def nt(left, right):
    return lax.dot_general(left, right, (((1,), (1,)), ((), ())), preferred_element_type=F32)


def tn(left, right):
    return lax.dot_general(left, right, (((0,), (0,)), ((), ())), preferred_element_type=F32)


def block128(index):
    return pl.ds(pl.multiple_of(index * 128, 128), 128)


def kernel(
    length_ref,
    context_hbm,
    gain_hbm,
    residual,
    out_weight,
    key_weight,
    value_weight,
    video_query,
    video_key,
    video_value,
    out_cotangent,
    attended,
    query_grad,
    key_grad,
    value_grad,
    key_weight_grad,
    value_weight_grad,
    q,
    k,
    v,
    do,
    out,
    dq,
    dk,
    dv,
    dk_total,
    dv_total,
    w_out,
    res,
    summed,
    part,
    part_in,
    piece,
    landed,
    text,
    text_t,
    wkv,
    kv_own,
    kv_core,
    kv_core_in,
    kv_far,
    kv_far_in,
    dkv_all,
    grads,
    grads_in,
    grads_passed,
    grads_sum,
    total_grads,
    context,
    gain,
    in_s,
    in_r,
    out_s,
    out_r,
    w_s,
    w_r,
    rs_s,
    rs_r,
    load_sem,
    res_sem,
    ag_s,
    ag_r,
    kc_s,
    kc_r,
    kf_s,
    kf_r,
    dk_s,
    dk_r,
    wg_s,
    wg_r,
    grad_sem,
    small_sem,
):
    dp = lax.axis_index("dp")
    seq = lax.axis_index("seq")
    y_lo = dp // 16
    z = (dp // 2) % 8
    core = dp % 2

    def seq_of(d):
        return ((seq // 2 + d // 2) % 4) * 2 + (seq % 2 + d % 2) % 2

    def seq_peer(d):
        return (dp, seq_of(d))

    def group_peer(i, d):
        return (((y_lo + i // 2) % 2) * 16 + z * 2 + (core + i % 2) % 2, seq_of(d))

    def core_peer():
        return (dp + 1 - 2 * core, seq)

    def far_peer():
        return ((1 - y_lo) * 16 + z * 2 + core, seq)

    def z_peer(i):
        return (y_lo * 16 + ((z + i) % 8) * 2 + core, seq)

    def remote(src, dst, send, recv, peer):
        return pltpu.make_async_remote_copy(
            src_ref=src, dst_ref=dst, send_sem=send, recv_sem=recv, device_id=peer, device_id_type=MESH
        )

    def loop(low, high, step):
        def run(i, carry):
            step(i)
            return carry

        lax.fori_loop(low, high, run, 0)

    def each(low, high, step):
        for i in range(low, high):
            step(i)


    def w_load(d, half):
        columns = pl.ds(pl.multiple_of(half * 2048 + seq_of(d) * 256, 256), 256)
        return pltpu.make_async_copy(
            out_weight.at[:, columns], w_out.at[d, :, pl.ds(half * 256, 256)], load_sem.at[d, half]
        )

    def res_load(half):
        columns = pl.ds(pl.multiple_of(half * 2048 + seq * 256, 256), 256)
        return pltpu.make_async_copy(
            residual.at[:, columns], res.at[:, pl.ds(half * 256, 256)], res_sem.at[half]
        )

    def weight_copy(n, h, i):
        return remote(
            (key_weight, value_weight)[n].at[:, block128(h)],
            wkv.at[h, z, :, pl.ds(n * 128, 128)],
            w_s.at[n, h, i],
            w_r.at[n, h, i],
            z_peer(i),
        )

    def weight_own(n, h):
        return pltpu.make_async_copy(
            (key_weight, value_weight)[n].at[:, block128(h)],
            wkv.at[h, z, :, pl.ds(n * 128, 128)],
            w_r.at[n, h, 0],
        )

    sources = (video_query, video_key, video_value, out_cotangent)
    landings = (q, k, v, do)
    results = (out, dq, dk, dv)
    targets = (attended, query_grad, key_grad, value_grad)

    def in_copy(n, h, d):
        peer = seq_peer(d)
        return remote(
            sources[n].at[:, block128(peer[1] * HEADS_HERE + h)],
            landings[n].at[h, block128(seq)],
            in_s.at[n, h],
            in_r.at[n, h],
            peer,
        )

    def in_own(n, h):
        return pltpu.make_async_copy(
            sources[n].at[:, block128(seq * HEADS_HERE + h)],
            landings[n].at[h, block128(seq)],
            in_r.at[n, h],
        )

    def out_copy(n, h, d):
        peer = seq_peer(d)
        return remote(
            results[n].at[h, block128(peer[1])],
            targets[n].at[:, block128(seq * HEADS_HERE + h)],
            out_s.at[n, h],
            out_r.at[n, h],
            peer,
        )

    def out_own(n, h):
        return pltpu.make_async_copy(
            results[n].at[h, block128(seq)],
            targets[n].at[:, block128(seq * HEADS_HERE + h)],
            out_r.at[n, h],
        )


    def all_in(n, h):
        rows = landings[n].at[h, pl.ds(0, TOKENS)]
        return pltpu.make_async_copy(rows, rows, in_r.at[n, h])

    def all_in_sent(n, h):
        rows = landings[n].at[h, pl.ds(0, TOKENS - ROWS)]
        return pltpu.make_async_copy(rows, rows, in_s.at[n, h])

    def all_out(n, h):
        rows = results[n].at[h]
        return pltpu.make_async_copy(rows, rows, out_r.at[n, h])

    def all_out_sent(n, h):
        rows = results[n].at[h, pl.ds(0, TOKENS - ROWS)]
        return pltpu.make_async_copy(rows, rows, out_s.at[n, h])

    def part_copy(d):
        return remote(part.at[d], part_in.at[d], rs_s.at[d], rs_r.at[d], seq_peer(d))

    def piece_copy(i, d):
        target = ((y_lo + i // 2) % 2) * 2 + (core + i % 2) % 2
        return remote(
            piece.at[target],
            landed.at[seq, (i % 2) * 2 + y_lo],
            ag_s.at[i, d],
            ag_r.at[i, d],
            group_peer(i, d),
        )

    def kv_core_copy(h):
        return remote(kv_core.at[h], kv_core_in.at[h], kc_s.at[h], kc_r.at[h], core_peer())

    def kv_far_copy(h):
        return remote(kv_far.at[h], kv_far_in.at[h], kf_s.at[h], kf_r.at[h], far_peer())

    def dkv_far(h):
        mine = dkv_all.at[h, y_lo]
        return remote(mine, mine, dk_s.at[h, 0], dk_r.at[h, 0], far_peer())

    def dkv_core(h, other):
        side = (1 - y_lo) if other else y_lo
        return remote(
            dkv_all.at[h, side],
            dkv_all.at[h, 2 + side],
            dk_s.at[h, 1 + other],
            dk_r.at[h, 1 + other],
            core_peer(),
        )

    def grad_near(h, n):
        step = (1, ZS - 1)[n]
        return remote(
            grads.at[h, (z + step) % 8], grads_in.at[h, n], wg_s.at[h, n], wg_r.at[h, n], z_peer(step)
        )

    def grad_passed(h, n):
        block, step = ((3, 1), (ZS - 3, ZS - 1), (4, 2))[n]
        return remote(
            grads.at[h, (z + block) % 8],
            grads_passed.at[h, n],
            wg_s.at[h, 2 + n],
            wg_r.at[h, 2 + n],
            z_peer(step),
        )

    def grad_far(h, n):
        step = (2, ZS - 2)[n]
        return remote(
            grads_sum.at[h, n], grads_in.at[h, 2 + n], wg_s.at[h, 5 + n], wg_r.at[h, 5 + n], z_peer(step)
        )

    def send_head_in(h):
        for n in range(4):
            each(1, SEQ, lambda d: in_copy(n, h, d).start())

    def all_group(step):
        each(1, SEQ, lambda d: step(0, d))
        each(1, GROUP, lambda i: each(0, SEQ, lambda d: step(i, d)))


    barrier = pltpu.get_barrier_semaphore()

    def greet(peer):
        pl.semaphore_signal(barrier, inc=1, device_id=peer, device_id_type=MESH)

    all_group(lambda i, d: greet(group_peer(i, d)))
    each(1, ZS, lambda i: greet(z_peer(i)))

    context_load = pltpu.make_async_copy(context_hbm, context, small_sem.at[0])
    gain_load = pltpu.make_async_copy(gain_hbm, gain, small_sem.at[1])
    context_load.start()

    def start_loads(d):
        for half in range(2):
            w_load(d, half).start()

    each(0, SEQ, start_loads)
    for half in range(2):
        res_load(half).start()
    gain_load.start()
    for h in range(HEADS_HERE):
        for n in range(2):
            weight_own(n, h).start()
        for n in range(4):
            in_own(n, h).start()


    def project(d):
        for half in range(2):
            w_load(d, half).wait()
        return nn(context[...], w_out[d])

    context_load.wait()
    gain_load.wait()
    for half in range(2):
        res_load(half).wait()
    summed[...] = project(0) + res[...].astype(F32)

    def project_step(d):
        part[d] = project(d).astype(BF)

    each(1, SEQ, project_step)
    pl.semaphore_wait(barrier, GROUP * SEQ - 1 + ZS - 1)
    each(1, SEQ, lambda d: part_copy(d).start())

    def send_weights(h):
        for n in range(2):
            each(1, ZS, lambda i: weight_copy(n, h, i).start())

    send_weights(0)
    send_head_in(0)
    send_weights(1)
    send_weights(2)

    for d in range(1, SEQ):
        part_copy(d).wait_recv()
        summed[...] += part_in[d].astype(F32)
    total = summed[...]
    square = lax.dot_general(
        jnp.ones((16, SHARE), F32),
        total * total,
        (((1,), (1,)), ((), ())),
        precision=lax.Precision.HIGHEST,
        preferred_element_type=F32,
    )
    high = square.astype(BF).astype(F32)
    middle = (square - high).astype(BF).astype(F32)
    low = square - high - middle
    row = lax.broadcasted_iota(jnp.int32, (16, PROMPT), 0)
    square_rows = jnp.where(
        row == 0, high, jnp.where(row == 1, middle, jnp.where(row == 2, low, 0.0))
    ).astype(BF)
    for half in range(2):
        columns = pl.ds(pl.multiple_of(half * 2048 + seq * 256, 256), 256)
        scaled = (total[:, half * 256 : (half + 1) * 256] * gain[:, columns]).astype(BF)
        for c in range(2):
            piece[half * 2 + c, :PROMPT, :] = scaled[:, c * 128 : (c + 1) * 128]
            piece[half * 2 + c, PROMPT:, :] = square_rows
    all_group(lambda i, d: piece_copy(i, d).start())
    landed[seq, y_lo] = piece[y_lo * 2 + core]
    send_head_in(1)


    all_group(lambda i, d: piece_copy(i, d).wait_recv())
    for g in range(GROUP):
        rows = landed[0, g, PROMPT:, :].astype(F32)
        for s in range(1, SEQ):
            rows = rows + landed[s, g, PROMPT:, :].astype(F32)
        mean = jnp.sum(rows, axis=0, keepdims=True) * (1.0 / D_TEXT)
        inverse = lax.rsqrt(jnp.transpose(jnp.broadcast_to(mean, (128, 128))) + EPSILON)
        for s in range(SEQ):
            text[g * 128 : (g + 1) * 128, s * 128 : (s + 1) * 128] = (
                landed[s, g, :PROMPT, :].astype(F32) * inverse
            ).astype(BF)


    def project_kv(h):
        def arrived(i):
            for n in range(2):
                weight_copy(n, h, i).wait_recv()

        each(1, ZS, arrived)
        for n in range(2):
            weight_own(n, h).wait()
        weights = wkv[h].reshape(ZS * 128, 256)
        kv_core[h] = nn(text[256:, :], weights).astype(BF)
        kv_core_copy(h).start()
        kv_own[h] = nn(text[:256, :], weights)

    def add_core(h):
        kv_core_copy(h).wait_recv()
        kv_own[h] += kv_core_in[h].astype(F32)
        kv_far[h] = kv_own[h, block128(1 - y_lo), :].astype(BF)
        kv_far_copy(h).start()

    loop(0, HEADS_HERE, project_kv)
    loop(0, HEADS_HERE, add_core)
    send_head_in(2)
    for g in range(GROUP):
        text_t[:, g * 128 : (g + 1) * 128] = jnp.transpose(text[g * 128 : (g + 1) * 128, :])


    length = length_ref[0]

    def attend(h, i):
        rows = pl.ds(pl.multiple_of(i * QUERY_BLOCK, QUERY_BLOCK), QUERY_BLOCK)
        queries, cotangent, keys, values = q[h, rows, :], do[h, rows, :], k[h], v[h]
        scores = nt(queries, keys)
        allowed = lax.broadcasted_iota(jnp.int32, (1, PROMPT), 1) < length
        scores = jnp.concatenate(
            [scores[:, :TOKENS], jnp.where(allowed, scores[:, TOKENS:], -jnp.inf)], axis=1
        )
        peak = jnp.max(scores, axis=1, keepdims=True)
        weights = jnp.exp2((scores - peak) * EXP2_SCALE)
        weights_low = weights.astype(BF)
        sums = nn(weights_low, jnp.concatenate([values, jnp.ones_like(values)], axis=1))
        inverse = 1.0 / sums[:, HEAD_DIM:]
        output = sums[:, :HEAD_DIM] * inverse
        out[h, rows, :] = output.astype(BF)
        cotangent_wide = cotangent.astype(F32)
        center = jnp.sum(cotangent_wide * output, axis=1, keepdims=True)
        score_grad = (weights * (nt(cotangent, values) - center)).astype(BF)
        scaled = inverse * SCALE
        dq[h, rows, :] = (nn(score_grad, keys) * scaled).astype(BF)
        dk_total[...] += tn(score_grad, (queries.astype(F32) * scaled).astype(BF))
        dv_total[...] += tn(weights_low, (cotangent_wide * inverse).astype(BF))

    def dkv_forward(h):
        dkv_far(h).wait_recv()
        dkv_core(h, 1).start()

    def weight_grads(h):
        dkv_core(h, 0).wait_recv()
        dkv_core(h, 1).wait_recv()
        products = nn(text_t[...], dkv_all[h].reshape(GROUP * 128, 256))
        grads[h] = products.astype(BF).reshape(ZS, 128, 256)
        for n in range(3):
            grad_passed(h, n).start()
        for n in range(2):
            grad_near(h, n).start()


    def pass_grads(h):
        for n in range(3):
            grad_passed(h, n).wait_recv()
        up = grads[h, (z + 2) % 8].astype(F32) + grads_passed[h, 0].astype(F32)
        grads_sum[h, 0] = (up + grads_passed[h, 2].astype(F32)).astype(BF)
        down = grads[h, (z + ZS - 2) % 8].astype(F32) + grads_passed[h, 1].astype(F32)
        grads_sum[h, 1] = down.astype(BF)
        for n in range(2):
            grad_far(h, n).start()

    def head(h):
        kv_far_copy(h).wait_recv()
        kv = kv_own[h, block128(y_lo), :] + kv_far_in[h].astype(F32)
        k[h, TOKENS:, :] = kv[:, :128].astype(BF)
        v[h, TOKENS:, :] = kv[:, 128:].astype(BF)
        for n in range(4):
            all_in(n, h).wait()
        dk_total[...] = jnp.zeros_like(dk_total)
        dv_total[...] = jnp.zeros_like(dv_total)
        attend(h, 0)

        @pl.when(h > 0)
        def _():
            dkv_forward(h - 1)

        attend(h, 1)
        dk[h] = dk_total[:TOKENS, :].astype(BF)
        dv[h] = dv_total[:TOKENS, :].astype(BF)
        dkv_all[h, y_lo] = jnp.concatenate(
            [dk_total[TOKENS:, :], dv_total[TOKENS:, :]], axis=1
        ).astype(BF)
        dkv_far(h).start()
        dkv_core(h, 0).start()
        for n in range(4):
            each(1, SEQ, lambda d: out_copy(n, h, d).start())
            out_own(n, h).start()

        @pl.when(h > 0)
        def _():
            weight_grads(h - 1)

        @pl.when(h > 1)
        def _():
            pass_grads(h - 2)

    loop(0, HEADS_HERE, head)
    dkv_forward(HEADS_HERE - 1)
    pass_grads(HEADS_HERE - 2)
    weight_grads(HEADS_HERE - 1)
    pass_grads(HEADS_HERE - 1)

    def grads_out(n):
        return pltpu.make_async_copy(
            total_grads.at[n], (key_weight_grad, value_weight_grad)[n], grad_sem.at[n]
        )

    for h in range(HEADS_HERE):
        total = grads[h, z].astype(F32)
        for n in range(2):
            grad_near(h, n).wait_recv()
            grad_far(h, n).wait_recv()
            total = total + grads_in[h, n].astype(F32) + grads_in[h, 2 + n].astype(F32)
        for n in range(2):
            total_grads[n, :, h * 128 : (h + 1) * 128] = total[:, n * 128 : (n + 1) * 128]
    for n in range(2):
        grads_out(n).start()


    def finish(h):
        for n in range(4):
            all_out(n, h).wait()
            all_out_sent(n, h).wait()
            all_in_sent(n, h).wait()
        kv_core_copy(h).wait_send()
        kv_far_copy(h).wait_send()
        dkv_far(h).wait_send()
        dkv_core(h, 0).wait_send()
        dkv_core(h, 1).wait_send()

        for n in range(3):
            grad_passed(h, n).wait_send()
        for n in range(2):
            grad_near(h, n).wait_send()
            grad_far(h, n).wait_send()

        def finish_z(i):
            for n in range(2):
                weight_copy(n, h, i).wait_send()

        each(1, ZS, finish_z)

    loop(0, HEADS_HERE, finish)
    each(1, SEQ, lambda d: part_copy(d).wait_send())
    all_group(lambda i, d: piece_copy(i, d).wait_send())
    for n in range(2):
        grads_out(n).wait()


def hand_over(*refs):
    count = 6
    sources, targets, holds = refs[:count], refs[count : 2 * count], refs[2 * count : 3 * count]
    sem = refs[3 * count]
    parts = [(n, part) for part in range(2) for n in range(count)]

    def load(n, part):
        rows = pl.ds(part * 64, 64)
        return pltpu.make_async_copy(sources[n].at[rows], holds[n].at[rows], sem.at[0, n, part])

    def store(n, part):
        rows = pl.ds(part * 64, 64)
        return pltpu.make_async_copy(holds[n].at[rows], targets[n].at[rows], sem.at[1, n, part])

    for n, part in parts:
        load(n, part).start()
    for n, part in parts:
        load(n, part).wait()
        store(n, part).start()
    for n, part in parts:
        store(n, part).wait()


def body(
    text_context,
    text_residual,
    text_out_weight,
    text_gain,
    prompt_length,
    key_weight,
    value_weight,
    video_query,
    video_key,
    video_value,
    out_cotangent,
):
    hbm = pl.BlockSpec(memory_space=pl.ANY)
    smem = pl.BlockSpec(memory_space=pltpu.SMEM)
    dma = pltpu.SemaphoreType.DMA
    tokens = jax.ShapeDtypeStruct((ROWS, SEQ * WIDTH), BF)
    weights = jax.ShapeDtypeStruct((128, WIDTH), F32)
    scratch = [
        pltpu.VMEM((HEADS_HERE, TOKENS, HEAD_DIM), BF),
        pltpu.VMEM((HEADS_HERE, ALL_ROWS, HEAD_DIM), BF),
        pltpu.VMEM((HEADS_HERE, ALL_ROWS, HEAD_DIM), BF),
        pltpu.VMEM((HEADS_HERE, TOKENS, HEAD_DIM), BF),
        pltpu.VMEM((HEADS_HERE, TOKENS, HEAD_DIM), BF),
        pltpu.VMEM((HEADS_HERE, TOKENS, HEAD_DIM), BF),
        pltpu.VMEM((HEADS_HERE, TOKENS, HEAD_DIM), BF),
        pltpu.VMEM((HEADS_HERE, TOKENS, HEAD_DIM), BF),
        pltpu.VMEM((ALL_ROWS, HEAD_DIM), F32),
        pltpu.VMEM((ALL_ROWS, HEAD_DIM), F32),
        pltpu.VMEM((SEQ, SHARE, SHARE), BF),
        pltpu.VMEM((PROMPT, SHARE), BF),
        pltpu.VMEM((PROMPT, SHARE), F32),
        pltpu.VMEM((SEQ, PROMPT, SHARE), BF),
        pltpu.VMEM((SEQ, PROMPT, SHARE), BF),
        pltpu.VMEM((GROUP, PROMPT + 16, 128), BF),
        pltpu.VMEM((SEQ, GROUP, PROMPT + 16, 128), BF),
        pltpu.VMEM((GROUP * PROMPT, SEQ * 128), BF),
        pltpu.VMEM((SEQ * 128, GROUP * PROMPT), BF),
        pltpu.VMEM((HEADS_HERE, ZS, 128, 256), BF),
        pltpu.VMEM((HEADS_HERE, 2 * PROMPT, 256), F32),
        pltpu.VMEM((HEADS_HERE, 2 * PROMPT, 256), BF),
        pltpu.VMEM((HEADS_HERE, 2 * PROMPT, 256), BF),
        pltpu.VMEM((HEADS_HERE, PROMPT, 256), BF),
        pltpu.VMEM((HEADS_HERE, PROMPT, 256), BF),
        pltpu.VMEM((HEADS_HERE, GROUP, PROMPT, 256), BF),
        pltpu.VMEM((HEADS_HERE, ZS, 128, 256), BF),
        pltpu.VMEM((HEADS_HERE, 4, 128, 256), BF),
        pltpu.VMEM((HEADS_HERE, 3, 128, 256), BF),
        pltpu.VMEM((HEADS_HERE, 2, 128, 256), BF),
        pltpu.VMEM((2, 128, WIDTH), F32),
        pltpu.VMEM((PROMPT, SHARE), BF),
        pltpu.VMEM((1, D_TEXT), F32),
        dma((4, HEADS_HERE)),
        dma((4, HEADS_HERE)),
        dma((4, HEADS_HERE)),
        dma((4, HEADS_HERE)),
        dma((2, HEADS_HERE, ZS)),
        dma((2, HEADS_HERE, ZS)),
        dma((SEQ,)),
        dma((SEQ,)),
        dma((SEQ, 2)),
        dma((2,)),
        dma((GROUP, SEQ)),
        dma((GROUP, SEQ)),
        dma((HEADS_HERE,)),
        dma((HEADS_HERE,)),
        dma((HEADS_HERE,)),
        dma((HEADS_HERE,)),
        dma((HEADS_HERE, 3)),
        dma((HEADS_HERE, 3)),
        dma((HEADS_HERE, 7)),
        dma((HEADS_HERE, 7)),
        dma((2,)),
        dma((2,)),
    ]
    shapes = [tokens] * 4 + [weights] * 2
    made = pl.pallas_call(
        kernel,
        out_shape=shapes,
        in_specs=[smem] + [hbm] * 10,
        out_specs=[hbm] * 6,
        scratch_shapes=scratch,
        name="joint_attention",
        compiler_params=pltpu.CompilerParams(
            collective_id=0, has_side_effects=True, vmem_limit_bytes=56 * 1024 * 1024
        ),
    )(
        prompt_length,
        text_context[0],
        text_gain.reshape(1, D_TEXT),
        text_residual[0],
        text_out_weight,
        key_weight,
        value_weight,
        video_query[0],
        video_key[0],
        video_value[0],
        out_cotangent[0],
    )
    attended, query_grad, key_grad, value_grad, key_weight_grad, value_weight_grad = pl.pallas_call(
        hand_over,
        out_shape=shapes,
        in_specs=[hbm] * 6,
        out_specs=[hbm] * 6,
        scratch_shapes=[pltpu.VMEM(x.shape, x.dtype) for x in shapes] + [dma((2, 6, 2))],
        name="hand_over",
    )(*made)
    return (
        attended[None],
        query_grad[None],
        key_grad[None],
        value_grad[None],
        key_weight_grad,
        value_weight_grad,
    )


def solution(mesh):
    in_specs = (
        P("dp", None, "seq"),
        P("dp", None, None),
        P("seq", None),
        P(),
        P("dp"),
        P("dp", "seq"),
        P("dp", "seq"),
        P("dp", "seq", None),
        P("dp", "seq", None),
        P("dp", "seq", None),
        P("dp", "seq", None),
    )
    out_specs = (
        P("dp", "seq", None),
        P("dp", "seq", None),
        P("dp", "seq", None),
        P("dp", "seq", None),
        P("dp", "seq"),
        P("dp", "seq"),
    )
    return jax.shard_map(body, mesh=mesh, in_specs=in_specs, out_specs=out_specs, check_vma=False)
```

```python
import math

import jax
import jax.numpy as jnp
from jax import lax
from jax.experimental import pallas as pl
from jax.experimental.pallas import tpu as pltpu
from jax.sharding import PartitionSpec as P

MESH = pl.DeviceIdType.MESH
BF = jnp.bfloat16
F32 = jnp.float32

HEAD_DIM = 128
EPSILON = 1e-06
SEQ = 8
ZS = 8
GROUP = 4
HEADS_HERE = 3
ROWS = 128
TOKENS = SEQ * ROWS
PROMPT = 128
ALL_ROWS = TOKENS + PROMPT
D_TEXT = 4096
SHARE = D_TEXT // SEQ
WIDTH = HEADS_HERE * HEAD_DIM
QUERY_BLOCK = 512
EXP2_SCALE = math.log2(math.e) / math.sqrt(HEAD_DIM)
SCALE = 1.0 / math.sqrt(HEAD_DIM)


def nn(left, right):
    return jnp.dot(left, right, preferred_element_type=F32)


def nt(left, right):
    return lax.dot_general(left, right, (((1,), (1,)), ((), ())), preferred_element_type=F32)


def tn(left, right):
    return lax.dot_general(left, right, (((0,), (0,)), ((), ())), preferred_element_type=F32)


def block128(index):
    return pl.ds(pl.multiple_of(index * 128, 128), 128)


def kernel(
    length_ref,
    context_hbm,
    gain_hbm,
    residual,
    out_weight,
    key_weight,
    value_weight,
    video_query,
    video_key,
    video_value,
    out_cotangent,
    attended,
    query_grad,
    key_grad,
    value_grad,
    key_weight_grad,
    value_weight_grad,
    q,
    k,
    v,
    do,
    out,
    dq,
    dk,
    dv,
    dk_total,
    dv_total,
    w_out,
    res,
    summed,
    part,
    part_in,
    piece,
    landed,
    text,
    text_t,
    wkv,
    kv_own,
    kv_core,
    kv_core_in,
    kv_far,
    kv_far_in,
    dkv_all,
    grads,
    grads_in,
    grads_passed,
    grads_sum,
    total_grads,
    context,
    gain,
    in_s,
    in_r,
    out_s,
    out_r,
    w_s,
    w_r,
    rs_s,
    rs_r,
    load_sem,
    res_sem,
    ag_s,
    ag_r,
    kc_s,
    kc_r,
    kf_s,
    kf_r,
    dk_s,
    dk_r,
    wg_s,
    wg_r,
    grad_sem,
    small_sem,
):
    dp = lax.axis_index("dp")
    seq = lax.axis_index("seq")
    y_lo = dp // 16
    z = (dp // 2) % 8
    core = dp % 2

    def seq_of(d):
        return ((seq // 2 + d // 2) % 4) * 2 + (seq % 2 + d % 2) % 2

    def seq_peer(d):
        return (dp, seq_of(d))

    def group_peer(i, d):
        return (((y_lo + i // 2) % 2) * 16 + z * 2 + (core + i % 2) % 2, seq_of(d))

    def core_peer():
        return (dp + 1 - 2 * core, seq)

    def far_peer():
        return ((1 - y_lo) * 16 + z * 2 + core, seq)

    def z_peer(i):
        return (y_lo * 16 + ((z + i) % 8) * 2 + core, seq)

    def remote(src, dst, send, recv, peer):
        return pltpu.make_async_remote_copy(
            src_ref=src, dst_ref=dst, send_sem=send, recv_sem=recv, device_id=peer, device_id_type=MESH
        )

    def loop(low, high, step):
        def run(i, carry):
            step(i)
            return carry

        lax.fori_loop(low, high, run, 0)

    def each(low, high, step):
        for i in range(low, high):
            step(i)


    def w_load(d, half):
        columns = pl.ds(pl.multiple_of(half * 2048 + seq_of(d) * 256, 256), 256)
        return pltpu.make_async_copy(
            out_weight.at[:, columns], w_out.at[d, :, pl.ds(half * 256, 256)], load_sem.at[d, half]
        )

    def res_load(half):
        columns = pl.ds(pl.multiple_of(half * 2048 + seq * 256, 256), 256)
        return pltpu.make_async_copy(
            residual.at[:, columns], res.at[:, pl.ds(half * 256, 256)], res_sem.at[half]
        )

    def weight_copy(n, h, i):
        return remote(
            (key_weight, value_weight)[n].at[:, block128(h)],
            wkv.at[h, z, :, pl.ds(n * 128, 128)],
            w_s.at[n, h, i],
            w_r.at[n, h, i],
            z_peer(i),
        )

    def weight_own(n, h):
        return pltpu.make_async_copy(
            (key_weight, value_weight)[n].at[:, block128(h)],
            wkv.at[h, z, :, pl.ds(n * 128, 128)],
            w_r.at[n, h, 0],
        )

    sources = (video_query, video_key, video_value, out_cotangent)
    landings = (q, k, v, do)
    results = (out, dq, dk, dv)
    targets = (attended, query_grad, key_grad, value_grad)

    def in_copy(n, h, d):
        peer = seq_peer(d)
        return remote(
            sources[n].at[:, block128(peer[1] * HEADS_HERE + h)],
            landings[n].at[h, block128(seq)],
            in_s.at[n, h],
            in_r.at[n, h],
            peer,
        )

    def in_own(n, h):
        return pltpu.make_async_copy(
            sources[n].at[:, block128(seq * HEADS_HERE + h)],
            landings[n].at[h, block128(seq)],
            in_r.at[n, h],
        )

    def out_copy(n, h, d):
        peer = seq_peer(d)
        return remote(
            results[n].at[h, block128(peer[1])],
            targets[n].at[:, block128(seq * HEADS_HERE + h)],
            out_s.at[n, h],
            out_r.at[n, h],
            peer,
        )

    def out_own(n, h):
        return pltpu.make_async_copy(
            results[n].at[h, block128(seq)],
            targets[n].at[:, block128(seq * HEADS_HERE + h)],
            out_r.at[n, h],
        )


    def all_in(n, h):
        rows = landings[n].at[h, pl.ds(0, TOKENS)]
        return pltpu.make_async_copy(rows, rows, in_r.at[n, h])

    def all_in_sent(n, h):
        rows = landings[n].at[h, pl.ds(0, TOKENS - ROWS)]
        return pltpu.make_async_copy(rows, rows, in_s.at[n, h])

    def all_out(n, h):
        rows = results[n].at[h]
        return pltpu.make_async_copy(rows, rows, out_r.at[n, h])

    def all_out_sent(n, h):
        rows = results[n].at[h, pl.ds(0, TOKENS - ROWS)]
        return pltpu.make_async_copy(rows, rows, out_s.at[n, h])

    def part_copy(d):
        return remote(part.at[d], part_in.at[d], rs_s.at[d], rs_r.at[d], seq_peer(d))

    def piece_copy(i, d):
        target = ((y_lo + i // 2) % 2) * 2 + (core + i % 2) % 2
        return remote(
            piece.at[target],
            landed.at[seq, (i % 2) * 2 + y_lo],
            ag_s.at[i, d],
            ag_r.at[i, d],
            group_peer(i, d),
        )

    def kv_core_copy(h):
        return remote(kv_core.at[h], kv_core_in.at[h], kc_s.at[h], kc_r.at[h], core_peer())

    def kv_far_copy(h):
        return remote(kv_far.at[h], kv_far_in.at[h], kf_s.at[h], kf_r.at[h], far_peer())

    def dkv_far(h):
        mine = dkv_all.at[h, y_lo]
        return remote(mine, mine, dk_s.at[h, 0], dk_r.at[h, 0], far_peer())

    def dkv_core(h, other):
        side = (1 - y_lo) if other else y_lo
        return remote(
            dkv_all.at[h, side],
            dkv_all.at[h, 2 + side],
            dk_s.at[h, 1 + other],
            dk_r.at[h, 1 + other],
            core_peer(),
        )

    def grad_near(h, n):
        step = (1, ZS - 1)[n]
        return remote(
            grads.at[h, (z + step) % 8], grads_in.at[h, n], wg_s.at[h, n], wg_r.at[h, n], z_peer(step)
        )

    def grad_passed(h, n):
        block, step, low, high = (
            (3, 1, 0, 128),
            (ZS - 3, ZS - 1, 0, 128),
            (4, 2, 0, 64),
            (4, ZS - 2, 64, 128),
        )[n]
        rows = pl.ds(low, high - low)
        return remote(
            grads.at[h, (z + block) % 8, rows],
            grads_passed.at[h, n, rows],
            wg_s.at[h, 2 + n],
            wg_r.at[h, 2 + n],
            z_peer(step),
        )

    def grad_far(h, n):
        step = (2, ZS - 2)[n]
        return remote(
            grads_sum.at[h, n], grads_in.at[h, 2 + n], wg_s.at[h, 6 + n], wg_r.at[h, 6 + n], z_peer(step)
        )

    def send_head_in(h):
        for n in range(4):
            each(1, SEQ, lambda d: in_copy(n, h, d).start())

    def all_group(step):
        each(1, SEQ, lambda d: step(0, d))
        each(1, GROUP, lambda i: each(0, SEQ, lambda d: step(i, d)))


    barrier = pltpu.get_barrier_semaphore()

    def greet(peer):
        pl.semaphore_signal(barrier, inc=1, device_id=peer, device_id_type=MESH)

    all_group(lambda i, d: greet(group_peer(i, d)))
    each(1, ZS, lambda i: greet(z_peer(i)))

    context_load = pltpu.make_async_copy(context_hbm, context, small_sem.at[0])
    gain_load = pltpu.make_async_copy(gain_hbm, gain, small_sem.at[1])
    context_load.start()

    def start_loads(d):
        for half in range(2):
            w_load(d, half).start()

    each(0, SEQ, start_loads)
    for half in range(2):
        res_load(half).start()
    gain_load.start()
    for h in range(HEADS_HERE):
        for n in range(2):
            weight_own(n, h).start()
        for n in range(4):
            in_own(n, h).start()


    def project(d):
        for half in range(2):
            w_load(d, half).wait()
        return nn(context[...], w_out[d])

    context_load.wait()
    gain_load.wait()
    for half in range(2):
        res_load(half).wait()
    summed[...] = project(0) + res[...].astype(F32)

    def project_step(d):
        part[d] = project(d).astype(BF)

    each(1, SEQ, project_step)
    pl.semaphore_wait(barrier, GROUP * SEQ - 1 + ZS - 1)
    each(1, SEQ, lambda d: part_copy(d).start())

    def send_weights(h):
        for n in range(2):
            each(1, ZS, lambda i: weight_copy(n, h, i).start())

    send_weights(0)
    send_head_in(0)
    send_weights(1)
    send_weights(2)

    for d in range(1, SEQ):
        part_copy(d).wait_recv()
        summed[...] += part_in[d].astype(F32)
    total = summed[...]
    square = lax.dot_general(
        jnp.ones((16, SHARE), F32),
        total * total,
        (((1,), (1,)), ((), ())),
        precision=lax.Precision.HIGHEST,
        preferred_element_type=F32,
    )
    high = square.astype(BF).astype(F32)
    middle = (square - high).astype(BF).astype(F32)
    low = square - high - middle
    row = lax.broadcasted_iota(jnp.int32, (16, PROMPT), 0)
    square_rows = jnp.where(
        row == 0, high, jnp.where(row == 1, middle, jnp.where(row == 2, low, 0.0))
    ).astype(BF)
    for half in range(2):
        columns = pl.ds(pl.multiple_of(half * 2048 + seq * 256, 256), 256)
        scaled = (total[:, half * 256 : (half + 1) * 256] * gain[:, columns]).astype(BF)
        for c in range(2):
            piece[half * 2 + c, :PROMPT, :] = scaled[:, c * 128 : (c + 1) * 128]
            piece[half * 2 + c, PROMPT:, :] = square_rows
    all_group(lambda i, d: piece_copy(i, d).start())
    landed[seq, y_lo] = piece[y_lo * 2 + core]
    send_head_in(1)


    all_group(lambda i, d: piece_copy(i, d).wait_recv())
    for g in range(GROUP):
        rows = landed[0, g, PROMPT:, :].astype(F32)
        for s in range(1, SEQ):
            rows = rows + landed[s, g, PROMPT:, :].astype(F32)
        mean = jnp.sum(rows, axis=0, keepdims=True) * (1.0 / D_TEXT)
        inverse = lax.rsqrt(jnp.transpose(jnp.broadcast_to(mean, (128, 128))) + EPSILON)
        for s in range(SEQ):
            text[g * 128 : (g + 1) * 128, s * 128 : (s + 1) * 128] = (
                landed[s, g, :PROMPT, :].astype(F32) * inverse
            ).astype(BF)


    def project_kv(h):
        def arrived(i):
            for n in range(2):
                weight_copy(n, h, i).wait_recv()

        each(1, ZS, arrived)
        for n in range(2):
            weight_own(n, h).wait()
        weights = wkv[h].reshape(ZS * 128, 256)
        kv_core[h] = nn(text[256:, :], weights).astype(BF)
        kv_core_copy(h).start()
        kv_own[h] = nn(text[:256, :], weights)

    def add_core(h):
        kv_core_copy(h).wait_recv()
        kv_own[h] += kv_core_in[h].astype(F32)
        kv_far[h] = kv_own[h, block128(1 - y_lo), :].astype(BF)
        kv_far_copy(h).start()

    loop(0, HEADS_HERE, project_kv)
    loop(0, HEADS_HERE, add_core)
    send_head_in(2)
    for g in range(GROUP):
        text_t[:, g * 128 : (g + 1) * 128] = jnp.transpose(text[g * 128 : (g + 1) * 128, :])


    length = length_ref[0]

    def attend(h, i):
        rows = pl.ds(pl.multiple_of(i * QUERY_BLOCK, QUERY_BLOCK), QUERY_BLOCK)
        queries, cotangent, keys, values = q[h, rows, :], do[h, rows, :], k[h], v[h]
        scores = nt(queries, keys)
        allowed = lax.broadcasted_iota(jnp.int32, (1, PROMPT), 1) < length
        scores = jnp.concatenate(
            [scores[:, :TOKENS], jnp.where(allowed, scores[:, TOKENS:], -jnp.inf)], axis=1
        )
        peak = jnp.max(scores, axis=1, keepdims=True)
        weights = jnp.exp2((scores - peak) * EXP2_SCALE)
        weights_low = weights.astype(BF)
        sums = nn(weights_low, jnp.concatenate([values, jnp.ones_like(values)], axis=1))
        inverse = 1.0 / sums[:, HEAD_DIM:]
        output = sums[:, :HEAD_DIM] * inverse
        out[h, rows, :] = output.astype(BF)
        cotangent_wide = cotangent.astype(F32)
        center = jnp.sum(cotangent_wide * output, axis=1, keepdims=True)
        score_grad = (weights * (nt(cotangent, values) - center)).astype(BF)
        scaled = inverse * SCALE
        dq[h, rows, :] = (nn(score_grad, keys) * scaled).astype(BF)
        dk_total[...] += tn(score_grad, (queries.astype(F32) * scaled).astype(BF))
        dv_total[...] += tn(weights_low, (cotangent_wide * inverse).astype(BF))

    def dkv_forward(h):
        dkv_far(h).wait_recv()
        dkv_core(h, 1).start()

    def weight_grads(h):
        dkv_core(h, 0).wait_recv()
        dkv_core(h, 1).wait_recv()
        products = nn(text_t[...], dkv_all[h].reshape(GROUP * 128, 256))
        grads[h] = products.astype(BF).reshape(ZS, 128, 256)
        for n in range(4):
            grad_passed(h, n).start()
        for n in range(2):
            grad_near(h, n).start()


    def pass_grads(h):
        for n in range(4):
            grad_passed(h, n).wait_recv()
        up = grads[h, (z + 2) % 8].astype(F32) + grads_passed[h, 0].astype(F32)
        grads_sum[h, 0, :64] = (up[:64] + grads_passed[h, 2, :64].astype(F32)).astype(BF)
        grads_sum[h, 0, 64:] = up[64:].astype(BF)
        down = grads[h, (z + ZS - 2) % 8].astype(F32) + grads_passed[h, 1].astype(F32)
        grads_sum[h, 1, :64] = down[:64].astype(BF)
        grads_sum[h, 1, 64:] = (down[64:] + grads_passed[h, 3, 64:].astype(F32)).astype(BF)
        for n in range(2):
            grad_far(h, n).start()

    def send_head_out(h, arrays):
        for n in arrays:
            each(1, SEQ, lambda d: out_copy(n, h, d).start())
            out_own(n, h).start()

    def head(h):
        kv_far_copy(h).wait_recv()
        kv = kv_own[h, block128(y_lo), :] + kv_far_in[h].astype(F32)
        k[h, TOKENS:, :] = kv[:, :128].astype(BF)
        v[h, TOKENS:, :] = kv[:, 128:].astype(BF)
        for n in range(4):
            all_in(n, h).wait()
        dk_total[...] = jnp.zeros_like(dk_total)
        dv_total[...] = jnp.zeros_like(dv_total)
        attend(h, 0)

        @pl.when(h > 0)
        def _():
            dkv_forward(h - 1)

        attend(h, 1)
        dk[h] = dk_total[:TOKENS, :].astype(BF)
        dv[h] = dv_total[:TOKENS, :].astype(BF)
        dkv_all[h, y_lo] = jnp.concatenate(
            [dk_total[TOKENS:, :], dv_total[TOKENS:, :]], axis=1
        ).astype(BF)
        dkv_far(h).start()
        dkv_core(h, 0).start()

        @pl.when(h < HEADS_HERE - 1)
        def _():
            send_head_out(h, range(4))

        @pl.when(h < HEADS_HERE - 2)
        def _():
            send_head_out(h, range(4, 4))

        @pl.when(h > 0)
        def _():
            weight_grads(h - 1)

        @pl.when(h > 1)
        def _():
            pass_grads(h - 2)

    loop(0, HEADS_HERE, head)
    dkv_forward(HEADS_HERE - 1)
    send_head_out(HEADS_HERE - 1, range(4))
    weight_grads(HEADS_HERE - 1)
    pass_grads(HEADS_HERE - 2)
    pass_grads(HEADS_HERE - 1)

    def grads_out(n):
        return pltpu.make_async_copy(
            total_grads.at[n], (key_weight_grad, value_weight_grad)[n], grad_sem.at[n]
        )

    for h in range(HEADS_HERE):
        total = grads[h, z].astype(F32)
        for n in range(2):
            grad_near(h, n).wait_recv()
            grad_far(h, n).wait_recv()
            total = total + grads_in[h, n].astype(F32) + grads_in[h, 2 + n].astype(F32)
        for n in range(2):
            total_grads[n, :, h * 128 : (h + 1) * 128] = total[:, n * 128 : (n + 1) * 128]
    for n in range(2):
        grads_out(n).start()


    def finish(h):
        for n in range(4):
            all_out(n, h).wait()
            all_out_sent(n, h).wait()
            all_in_sent(n, h).wait()
        kv_core_copy(h).wait_send()
        kv_far_copy(h).wait_send()
        dkv_far(h).wait_send()
        dkv_core(h, 0).wait_send()
        dkv_core(h, 1).wait_send()

        for n in range(4):
            grad_passed(h, n).wait_send()
        for n in range(2):
            grad_near(h, n).wait_send()
            grad_far(h, n).wait_send()

        def finish_z(i):
            for n in range(2):
                weight_copy(n, h, i).wait_send()

        each(1, ZS, finish_z)

    loop(0, HEADS_HERE, finish)
    each(1, SEQ, lambda d: part_copy(d).wait_send())
    all_group(lambda i, d: piece_copy(i, d).wait_send())
    for n in range(2):
        grads_out(n).wait()


def hand_over(*refs):
    count = 6
    sources, targets, holds = refs[:count], refs[count : 2 * count], refs[2 * count : 3 * count]
    sem = refs[3 * count]
    parts = [(n, part) for part in range(2) for n in range(count)]

    def load(n, part):
        rows = pl.ds(part * 64, 64)
        return pltpu.make_async_copy(sources[n].at[rows], holds[n].at[rows], sem.at[0, n, part])

    def store(n, part):
        rows = pl.ds(part * 64, 64)
        return pltpu.make_async_copy(holds[n].at[rows], targets[n].at[rows], sem.at[1, n, part])

    for n, part in parts:
        load(n, part).start()
    for n, part in parts:
        load(n, part).wait()
        store(n, part).start()
    for n, part in parts:
        store(n, part).wait()


def body(
    text_context,
    text_residual,
    text_out_weight,
    text_gain,
    prompt_length,
    key_weight,
    value_weight,
    video_query,
    video_key,
    video_value,
    out_cotangent,
):
    hbm = pl.BlockSpec(memory_space=pl.ANY)
    smem = pl.BlockSpec(memory_space=pltpu.SMEM)
    dma = pltpu.SemaphoreType.DMA
    tokens = jax.ShapeDtypeStruct((ROWS, SEQ * WIDTH), BF)
    weights = jax.ShapeDtypeStruct((128, WIDTH), F32)
    scratch = [
        pltpu.VMEM((HEADS_HERE, TOKENS, HEAD_DIM), BF),
        pltpu.VMEM((HEADS_HERE, ALL_ROWS, HEAD_DIM), BF),
        pltpu.VMEM((HEADS_HERE, ALL_ROWS, HEAD_DIM), BF),
        pltpu.VMEM((HEADS_HERE, TOKENS, HEAD_DIM), BF),
        pltpu.VMEM((HEADS_HERE, TOKENS, HEAD_DIM), BF),
        pltpu.VMEM((HEADS_HERE, TOKENS, HEAD_DIM), BF),
        pltpu.VMEM((HEADS_HERE, TOKENS, HEAD_DIM), BF),
        pltpu.VMEM((HEADS_HERE, TOKENS, HEAD_DIM), BF),
        pltpu.VMEM((ALL_ROWS, HEAD_DIM), F32),
        pltpu.VMEM((ALL_ROWS, HEAD_DIM), F32),
        pltpu.VMEM((SEQ, SHARE, SHARE), BF),
        pltpu.VMEM((PROMPT, SHARE), BF),
        pltpu.VMEM((PROMPT, SHARE), F32),
        pltpu.VMEM((SEQ, PROMPT, SHARE), BF),
        pltpu.VMEM((SEQ, PROMPT, SHARE), BF),
        pltpu.VMEM((GROUP, PROMPT + 16, 128), BF),
        pltpu.VMEM((SEQ, GROUP, PROMPT + 16, 128), BF),
        pltpu.VMEM((GROUP * PROMPT, SEQ * 128), BF),
        pltpu.VMEM((SEQ * 128, GROUP * PROMPT), BF),
        pltpu.VMEM((HEADS_HERE, ZS, 128, 256), BF),
        pltpu.VMEM((HEADS_HERE, 2 * PROMPT, 256), F32),
        pltpu.VMEM((HEADS_HERE, 2 * PROMPT, 256), BF),
        pltpu.VMEM((HEADS_HERE, 2 * PROMPT, 256), BF),
        pltpu.VMEM((HEADS_HERE, PROMPT, 256), BF),
        pltpu.VMEM((HEADS_HERE, PROMPT, 256), BF),
        pltpu.VMEM((HEADS_HERE, GROUP, PROMPT, 256), BF),
        pltpu.VMEM((HEADS_HERE, ZS, 128, 256), BF),
        pltpu.VMEM((HEADS_HERE, 4, 128, 256), BF),
        pltpu.VMEM((HEADS_HERE, 4, 128, 256), BF),
        pltpu.VMEM((HEADS_HERE, 2, 128, 256), BF),
        pltpu.VMEM((2, 128, WIDTH), F32),
        pltpu.VMEM((PROMPT, SHARE), BF),
        pltpu.VMEM((1, D_TEXT), F32),
        dma((4, HEADS_HERE)),
        dma((4, HEADS_HERE)),
        dma((4, HEADS_HERE)),
        dma((4, HEADS_HERE)),
        dma((2, HEADS_HERE, ZS)),
        dma((2, HEADS_HERE, ZS)),
        dma((SEQ,)),
        dma((SEQ,)),
        dma((SEQ, 2)),
        dma((2,)),
        dma((GROUP, SEQ)),
        dma((GROUP, SEQ)),
        dma((HEADS_HERE,)),
        dma((HEADS_HERE,)),
        dma((HEADS_HERE,)),
        dma((HEADS_HERE,)),
        dma((HEADS_HERE, 3)),
        dma((HEADS_HERE, 3)),
        dma((HEADS_HERE, 8)),
        dma((HEADS_HERE, 8)),
        dma((2,)),
        dma((2,)),
    ]
    shapes = [tokens] * 4 + [weights] * 2
    made = pl.pallas_call(
        kernel,
        out_shape=shapes,
        in_specs=[smem] + [hbm] * 10,
        out_specs=[hbm] * 6,
        scratch_shapes=scratch,
        name="joint_attention",
        compiler_params=pltpu.CompilerParams(
            collective_id=0, has_side_effects=True, vmem_limit_bytes=56 * 1024 * 1024
        ),
    )(
        prompt_length,
        text_context[0],
        text_gain.reshape(1, D_TEXT),
        text_residual[0],
        text_out_weight,
        key_weight,
        value_weight,
        video_query[0],
        video_key[0],
        video_value[0],
        out_cotangent[0],
    )
    attended, query_grad, key_grad, value_grad, key_weight_grad, value_weight_grad = pl.pallas_call(
        hand_over,
        out_shape=shapes,
        in_specs=[hbm] * 6,
        out_specs=[hbm] * 6,
        scratch_shapes=[pltpu.VMEM(x.shape, x.dtype) for x in shapes] + [dma((2, 6, 2))],
        name="hand_over",
    )(*made)
    return (
        attended[None],
        query_grad[None],
        key_grad[None],
        value_grad[None],
        key_weight_grad,
        value_weight_grad,
    )


def solution(mesh):
    in_specs = (
        P("dp", None, "seq"),
        P("dp", None, None),
        P("seq", None),
        P(),
        P("dp"),
        P("dp", "seq"),
        P("dp", "seq"),
        P("dp", "seq", None),
        P("dp", "seq", None),
        P("dp", "seq", None),
        P("dp", "seq", None),
    )
    out_specs = (
        P("dp", "seq", None),
        P("dp", "seq", None),
        P("dp", "seq", None),
        P("dp", "seq", None),
        P("dp", "seq"),
        P("dp", "seq"),
    )
    return jax.shard_map(body, mesh=mesh, in_specs=in_specs, out_specs=out_specs, check_vma=False)
```

```python
import math

import jax
import jax.numpy as jnp
from jax import lax
from jax.experimental import pallas as pl
from jax.experimental.pallas import tpu as pltpu
from jax.sharding import PartitionSpec as P

MESH = pl.DeviceIdType.MESH
BF = jnp.bfloat16
F32 = jnp.float32

HEAD_DIM = 128
EPSILON = 1e-06
SEQ = 8
ZS = 8
GROUP = 4
HEADS_HERE = 3
ROWS = 128
TOKENS = SEQ * ROWS
PROMPT = 128
ALL_ROWS = TOKENS + PROMPT
D_TEXT = 4096
SHARE = D_TEXT // SEQ
WIDTH = HEADS_HERE * HEAD_DIM
QUERY_BLOCK = 512
EXP2_SCALE = math.log2(math.e) / math.sqrt(HEAD_DIM)
SCALE = 1.0 / math.sqrt(HEAD_DIM)


def nn(left, right):
    return jnp.dot(left, right, preferred_element_type=F32)


def nt(left, right):
    return lax.dot_general(left, right, (((1,), (1,)), ((), ())), preferred_element_type=F32)


def tn(left, right):
    return lax.dot_general(left, right, (((0,), (0,)), ((), ())), preferred_element_type=F32)


def block128(index):
    return pl.ds(pl.multiple_of(index * 128, 128), 128)


def kernel(
    length_ref,
    context_hbm,
    gain_hbm,
    residual,
    out_weight,
    key_weight,
    value_weight,
    video_query,
    video_key,
    video_value,
    out_cotangent,
    attended,
    query_grad,
    key_grad,
    value_grad,
    key_weight_grad,
    value_weight_grad,
    q,
    k,
    v,
    do,
    out,
    dq,
    dk,
    dv,
    dk_total,
    dv_total,
    w_out,
    res,
    summed,
    part,
    part_in,
    piece,
    landed,
    text,
    text_t,
    wkv,
    kv_own,
    kv_core,
    kv_core_in,
    kv_far,
    kv_far_in,
    dkv_all,
    grads,
    grads_in,
    grads_passed,
    grads_sum,
    total_grads,
    context,
    gain,
    in_s,
    in_r,
    out_s,
    out_r,
    w_s,
    w_r,
    rs_s,
    rs_r,
    load_sem,
    res_sem,
    ag_s,
    ag_r,
    kc_s,
    kc_r,
    kf_s,
    kf_r,
    dk_s,
    dk_r,
    wg_s,
    wg_r,
    grad_sem,
    small_sem,
):
    dp = lax.axis_index("dp")
    seq = lax.axis_index("seq")
    y_lo = dp // 16
    z = (dp // 2) % 8
    core = dp % 2

    def seq_of(d):
        return ((seq // 2 + d // 2) % 4) * 2 + (seq % 2 + d % 2) % 2

    def seq_peer(d):
        return (dp, seq_of(d))

    def group_peer(i, d):
        return (((y_lo + i // 2) % 2) * 16 + z * 2 + (core + i % 2) % 2, seq_of(d))

    def core_peer():
        return (dp + 1 - 2 * core, seq)

    def far_peer():
        return ((1 - y_lo) * 16 + z * 2 + core, seq)

    def z_peer(i):
        return (y_lo * 16 + ((z + i) % 8) * 2 + core, seq)

    def remote(src, dst, send, recv, peer):
        return pltpu.make_async_remote_copy(
            src_ref=src, dst_ref=dst, send_sem=send, recv_sem=recv, device_id=peer, device_id_type=MESH
        )

    def loop(low, high, step):
        def run(i, carry):
            step(i)
            return carry

        lax.fori_loop(low, high, run, 0)

    def each(low, high, step):
        for i in range(low, high):
            step(i)


    def w_load(d, half):
        columns = pl.ds(pl.multiple_of(half * 2048 + seq_of(d) * 256, 256), 256)
        return pltpu.make_async_copy(
            out_weight.at[:, columns], w_out.at[d, :, pl.ds(half * 256, 256)], load_sem.at[d, half]
        )

    def res_load(half):
        columns = pl.ds(pl.multiple_of(half * 2048 + seq * 256, 256), 256)
        return pltpu.make_async_copy(
            residual.at[:, columns], res.at[:, pl.ds(half * 256, 256)], res_sem.at[half]
        )

    def weight_copy(n, h, i):
        return remote(
            (key_weight, value_weight)[n].at[:, block128(h)],
            wkv.at[h, z, :, pl.ds(n * 128, 128)],
            w_s.at[n, h, i],
            w_r.at[n, h, i],
            z_peer(i),
        )

    def weight_own(n, h):
        return pltpu.make_async_copy(
            (key_weight, value_weight)[n].at[:, block128(h)],
            wkv.at[h, z, :, pl.ds(n * 128, 128)],
            w_r.at[n, h, 0],
        )

    sources = (video_query, video_key, video_value, out_cotangent)
    landings = (q, k, v, do)
    results = (out, dq, dk, dv)
    targets = (attended, query_grad, key_grad, value_grad)

    def in_copy(n, h, d):
        peer = seq_peer(d)
        return remote(
            sources[n].at[:, block128(peer[1] * HEADS_HERE + h)],
            landings[n].at[h, block128(seq)],
            in_s.at[n, h],
            in_r.at[n, h],
            peer,
        )

    def in_own(n, h):
        return pltpu.make_async_copy(
            sources[n].at[:, block128(seq * HEADS_HERE + h)],
            landings[n].at[h, block128(seq)],
            in_r.at[n, h],
        )

    def out_copy(n, h, d):
        peer = seq_peer(d)
        return remote(
            results[n].at[h, block128(peer[1])],
            targets[n].at[:, block128(seq * HEADS_HERE + h)],
            out_s.at[n, h],
            out_r.at[n, h],
            peer,
        )

    def out_own(n, h):
        return pltpu.make_async_copy(
            results[n].at[h, block128(seq)],
            targets[n].at[:, block128(seq * HEADS_HERE + h)],
            out_r.at[n, h],
        )


    def all_in(n, h):
        rows = landings[n].at[h, pl.ds(0, TOKENS)]
        return pltpu.make_async_copy(rows, rows, in_r.at[n, h])

    def all_in_sent(n, h):
        rows = landings[n].at[h, pl.ds(0, TOKENS - ROWS)]
        return pltpu.make_async_copy(rows, rows, in_s.at[n, h])

    def all_out(n, h):
        rows = results[n].at[h]
        return pltpu.make_async_copy(rows, rows, out_r.at[n, h])

    def all_out_sent(n, h):
        rows = results[n].at[h, pl.ds(0, TOKENS - ROWS)]
        return pltpu.make_async_copy(rows, rows, out_s.at[n, h])

    def part_copy(d):
        return remote(part.at[d], part_in.at[d], rs_s.at[d], rs_r.at[d], seq_peer(d))

    def part_piece(d, c):
        rows = pl.ds(c * 32, 32)
        return remote(part.at[d, rows], part_in.at[d, rows], rs_s.at[d], rs_r.at[d], seq_peer(d))

    def piece_copy(i, d):
        target = ((y_lo + i // 2) % 2) * 2 + (core + i % 2) % 2
        return remote(
            piece.at[target],
            landed.at[seq, (i % 2) * 2 + y_lo],
            ag_s.at[i, d],
            ag_r.at[i, d],
            group_peer(i, d),
        )

    def kv_core_copy(h):
        return remote(kv_core.at[h], kv_core_in.at[h], kc_s.at[h], kc_r.at[h], core_peer())

    def kv_far_copy(h):
        return remote(kv_far.at[h], kv_far_in.at[h], kf_s.at[h], kf_r.at[h], far_peer())

    def dkv_far(h):
        mine = dkv_all.at[h, y_lo]
        return remote(mine, mine, dk_s.at[h, 0], dk_r.at[h, 0], far_peer())

    def dkv_core(h, other):
        side = (1 - y_lo) if other else y_lo
        return remote(
            dkv_all.at[h, side],
            dkv_all.at[h, 2 + side],
            dk_s.at[h, 1 + other],
            dk_r.at[h, 1 + other],
            core_peer(),
        )

    def grad_near(h, n):
        step = (1, ZS - 1)[n]
        return remote(
            grads.at[h, (z + step) % 8], grads_in.at[h, n], wg_s.at[h, n], wg_r.at[h, n], z_peer(step)
        )

    def grad_passed(h, n):
        block, step, low, high = (
            (3, 1, 0, 128),
            (ZS - 3, ZS - 1, 0, 128),
            (4, 2, 0, 64),
            (4, ZS - 2, 64, 128),
        )[n]
        rows = pl.ds(low, high - low)
        return remote(
            grads.at[h, (z + block) % 8, rows],
            grads_passed.at[h, n, rows],
            wg_s.at[h, 2 + n],
            wg_r.at[h, 2 + n],
            z_peer(step),
        )

    def grad_far(h, n):
        step = (2, ZS - 2)[n]
        return remote(
            grads_sum.at[h, n], grads_in.at[h, 2 + n], wg_s.at[h, 6 + n], wg_r.at[h, 6 + n], z_peer(step)
        )

    def send_head_in(h):
        for n in range(4):
            each(1, SEQ, lambda d: in_copy(n, h, d).start())

    def all_group(step):
        each(1, SEQ, lambda d: step(0, d))
        each(1, GROUP, lambda i: each(0, SEQ, lambda d: step(i, d)))


    barrier = pltpu.get_barrier_semaphore()

    def greet(peer):
        pl.semaphore_signal(barrier, inc=1, device_id=peer, device_id_type=MESH)

    all_group(lambda i, d: greet(group_peer(i, d)))
    each(1, ZS, lambda i: greet(z_peer(i)))

    context_load = pltpu.make_async_copy(context_hbm, context, small_sem.at[0])
    gain_load = pltpu.make_async_copy(gain_hbm, gain, small_sem.at[1])
    context_load.start()

    def start_loads(d):
        for half in range(2):
            w_load(d, half).start()

    each(0, SEQ, start_loads)
    for half in range(2):
        res_load(half).start()
    gain_load.start()
    for h in range(HEADS_HERE):
        for n in range(2):
            weight_own(n, h).start()
        for n in range(4):
            in_own(n, h).start()


    def project(d):
        for half in range(2):
            w_load(d, half).wait()
        return nn(context[...], w_out[d])

    context_load.wait()
    gain_load.wait()
    for half in range(2):
        res_load(half).wait()
    summed[...] = project(0) + res[...].astype(F32)

    def project_step(d):
        part[d] = project(d).astype(BF)

    each(1, SEQ, project_step)
    pl.semaphore_wait(barrier, GROUP * SEQ - 1 + ZS - 1)
    for c in range(4):
        each(1, SEQ, lambda d: part_piece(d, c).start())

    def send_weights(h):
        for n in range(2):
            each(1, ZS, lambda i: weight_copy(n, h, i).start())

    send_head_in(0)
    send_weights(0)
    send_weights(1)
    send_weights(2)

    for d in range(1, SEQ):
        part_copy(d).wait_recv()
        summed[...] += part_in[d].astype(F32)
    total = summed[...]
    square = lax.dot_general(
        jnp.ones((16, SHARE), F32),
        total * total,
        (((1,), (1,)), ((), ())),
        precision=lax.Precision.HIGHEST,
        preferred_element_type=F32,
    )
    high = square.astype(BF).astype(F32)
    middle = (square - high).astype(BF).astype(F32)
    low = square - high - middle
    row = lax.broadcasted_iota(jnp.int32, (16, PROMPT), 0)
    square_rows = jnp.where(
        row == 0, high, jnp.where(row == 1, middle, jnp.where(row == 2, low, 0.0))
    ).astype(BF)
    for half in range(2):
        columns = pl.ds(pl.multiple_of(half * 2048 + seq * 256, 256), 256)
        scaled = (total[:, half * 256 : (half + 1) * 256] * gain[:, columns]).astype(BF)
        for c in range(2):
            piece[half * 2 + c, :PROMPT, :] = scaled[:, c * 128 : (c + 1) * 128]
            piece[half * 2 + c, PROMPT:, :] = square_rows
    all_group(lambda i, d: piece_copy(i, d).start())
    landed[seq, y_lo] = piece[y_lo * 2 + core]
    send_head_in(1)


    all_group(lambda i, d: piece_copy(i, d).wait_recv())
    for g in range(GROUP):
        rows = landed[0, g, PROMPT:, :].astype(F32)
        for s in range(1, SEQ):
            rows = rows + landed[s, g, PROMPT:, :].astype(F32)
        mean = jnp.sum(rows, axis=0, keepdims=True) * (1.0 / D_TEXT)
        inverse = lax.rsqrt(jnp.transpose(jnp.broadcast_to(mean, (128, 128))) + EPSILON)
        for s in range(SEQ):
            text[g * 128 : (g + 1) * 128, s * 128 : (s + 1) * 128] = (
                landed[s, g, :PROMPT, :].astype(F32) * inverse
            ).astype(BF)


    def project_kv(h):
        def arrived(i):
            for n in range(2):
                weight_copy(n, h, i).wait_recv()

        each(1, ZS, arrived)
        for n in range(2):
            weight_own(n, h).wait()
        weights = wkv[h].reshape(ZS * 128, 256)
        kv_core[h] = nn(text[256:, :], weights).astype(BF)
        kv_core_copy(h).start()
        kv_own[h] = nn(text[:256, :], weights)

    def add_core(h):
        kv_core_copy(h).wait_recv()
        kv_own[h] += kv_core_in[h].astype(F32)
        kv_far[h] = kv_own[h, block128(1 - y_lo), :].astype(BF)
        kv_far_copy(h).start()

    loop(0, HEADS_HERE, project_kv)
    loop(0, HEADS_HERE, add_core)
    send_head_in(2)
    for g in range(GROUP):
        text_t[:, g * 128 : (g + 1) * 128] = jnp.transpose(text[g * 128 : (g + 1) * 128, :])


    length = length_ref[0]

    def attend(h, i):
        rows = pl.ds(pl.multiple_of(i * QUERY_BLOCK, QUERY_BLOCK), QUERY_BLOCK)
        queries, cotangent, keys, values = q[h, rows, :], do[h, rows, :], k[h], v[h]
        scores = nt(queries, keys)
        allowed = lax.broadcasted_iota(jnp.int32, (1, PROMPT), 1) < length
        scores = jnp.concatenate(
            [scores[:, :TOKENS], jnp.where(allowed, scores[:, TOKENS:], -jnp.inf)], axis=1
        )
        peak = jnp.max(scores, axis=1, keepdims=True)
        weights = jnp.exp2((scores - peak) * EXP2_SCALE)
        weights_low = weights.astype(BF)
        sums = nn(weights_low, jnp.concatenate([values, jnp.ones_like(values)], axis=1))
        inverse = 1.0 / sums[:, HEAD_DIM:]
        output = sums[:, :HEAD_DIM] * inverse
        out[h, rows, :] = output.astype(BF)
        cotangent_wide = cotangent.astype(F32)
        center = jnp.sum(cotangent_wide * output, axis=1, keepdims=True)
        score_grad = (weights * (nt(cotangent, values) - center)).astype(BF)
        scaled = inverse * SCALE
        dq[h, rows, :] = (nn(score_grad, keys) * scaled).astype(BF)
        dk_total[...] += tn(score_grad, (queries.astype(F32) * scaled).astype(BF))
        dv_total[...] += tn(weights_low, (cotangent_wide * inverse).astype(BF))

    def dkv_forward(h):
        dkv_far(h).wait_recv()
        dkv_core(h, 1).start()

    def weight_grads(h):
        dkv_core(h, 0).wait_recv()
        dkv_core(h, 1).wait_recv()
        products = nn(text_t[...], dkv_all[h].reshape(GROUP * 128, 256))
        grads[h] = products.astype(BF).reshape(ZS, 128, 256)
        for n in range(4):
            grad_passed(h, n).start()
        for n in range(2):
            grad_near(h, n).start()


    def pass_grads(h):
        for n in range(4):
            grad_passed(h, n).wait_recv()
        up = grads[h, (z + 2) % 8].astype(F32) + grads_passed[h, 0].astype(F32)
        grads_sum[h, 0, :64] = (up[:64] + grads_passed[h, 2, :64].astype(F32)).astype(BF)
        grads_sum[h, 0, 64:] = up[64:].astype(BF)
        down = grads[h, (z + ZS - 2) % 8].astype(F32) + grads_passed[h, 1].astype(F32)
        grads_sum[h, 1, :64] = down[:64].astype(BF)
        grads_sum[h, 1, 64:] = (down[64:] + grads_passed[h, 3, 64:].astype(F32)).astype(BF)
        for n in range(2):
            grad_far(h, n).start()

    def send_head_out(h, arrays):
        for n in arrays:
            each(1, SEQ, lambda d: out_copy(n, h, d).start())
            out_own(n, h).start()

    def head(h):
        kv_far_copy(h).wait_recv()
        kv = kv_own[h, block128(y_lo), :] + kv_far_in[h].astype(F32)
        k[h, TOKENS:, :] = kv[:, :128].astype(BF)
        v[h, TOKENS:, :] = kv[:, 128:].astype(BF)
        for n in range(4):
            all_in(n, h).wait()
        dk_total[...] = jnp.zeros_like(dk_total)
        dv_total[...] = jnp.zeros_like(dv_total)
        attend(h, 0)

        @pl.when(h > 0)
        def _():
            dkv_forward(h - 1)

        attend(h, 1)
        dk[h] = dk_total[:TOKENS, :].astype(BF)
        dv[h] = dv_total[:TOKENS, :].astype(BF)
        dkv_all[h, y_lo] = jnp.concatenate(
            [dk_total[TOKENS:, :], dv_total[TOKENS:, :]], axis=1
        ).astype(BF)
        dkv_far(h).start()
        dkv_core(h, 0).start()

        @pl.when(h < HEADS_HERE - 1)
        def _():
            send_head_out(h, range(4))

        @pl.when(h < HEADS_HERE - 2)
        def _():
            send_head_out(h, range(4, 4))

        @pl.when(h > 0)
        def _():
            weight_grads(h - 1)

        @pl.when(h > 1)
        def _():
            pass_grads(h - 2)

    loop(0, HEADS_HERE, head)
    dkv_forward(HEADS_HERE - 1)
    send_head_out(HEADS_HERE - 1, range(4))
    weight_grads(HEADS_HERE - 1)
    pass_grads(HEADS_HERE - 2)
    pass_grads(HEADS_HERE - 1)

    def grads_out(n):
        return pltpu.make_async_copy(
            total_grads.at[n], (key_weight_grad, value_weight_grad)[n], grad_sem.at[n]
        )

    for h in range(HEADS_HERE):
        total = grads[h, z].astype(F32)
        for n in range(2):
            grad_near(h, n).wait_recv()
            grad_far(h, n).wait_recv()
            total = total + grads_in[h, n].astype(F32) + grads_in[h, 2 + n].astype(F32)
        for n in range(2):
            total_grads[n, :, h * 128 : (h + 1) * 128] = total[:, n * 128 : (n + 1) * 128]
    for n in range(2):
        grads_out(n).start()


    def finish(h):
        for n in range(4):
            all_out(n, h).wait()
            all_out_sent(n, h).wait()
            all_in_sent(n, h).wait()
        kv_core_copy(h).wait_send()
        kv_far_copy(h).wait_send()
        dkv_far(h).wait_send()
        dkv_core(h, 0).wait_send()
        dkv_core(h, 1).wait_send()

        for n in range(4):
            grad_passed(h, n).wait_send()
        for n in range(2):
            grad_near(h, n).wait_send()
            grad_far(h, n).wait_send()

        def finish_z(i):
            for n in range(2):
                weight_copy(n, h, i).wait_send()

        each(1, ZS, finish_z)

    loop(0, HEADS_HERE, finish)
    each(1, SEQ, lambda d: part_copy(d).wait_send())
    all_group(lambda i, d: piece_copy(i, d).wait_send())
    for n in range(2):
        grads_out(n).wait()


def hand_over(*refs):
    count = 6
    sources, targets, holds = refs[:count], refs[count : 2 * count], refs[2 * count : 3 * count]
    sem = refs[3 * count]
    parts = [(n, part) for part in range(2) for n in range(count)]

    def load(n, part):
        rows = pl.ds(part * 64, 64)
        return pltpu.make_async_copy(sources[n].at[rows], holds[n].at[rows], sem.at[0, n, part])

    def store(n, part):
        rows = pl.ds(part * 64, 64)
        return pltpu.make_async_copy(holds[n].at[rows], targets[n].at[rows], sem.at[1, n, part])

    for n, part in parts:
        load(n, part).start()
    for n, part in parts:
        load(n, part).wait()
        store(n, part).start()
    for n, part in parts:
        store(n, part).wait()


def body(
    text_context,
    text_residual,
    text_out_weight,
    text_gain,
    prompt_length,
    key_weight,
    value_weight,
    video_query,
    video_key,
    video_value,
    out_cotangent,
):
    hbm = pl.BlockSpec(memory_space=pl.ANY)
    smem = pl.BlockSpec(memory_space=pltpu.SMEM)
    dma = pltpu.SemaphoreType.DMA
    tokens = jax.ShapeDtypeStruct((ROWS, SEQ * WIDTH), BF)
    weights = jax.ShapeDtypeStruct((128, WIDTH), F32)
    scratch = [
        pltpu.VMEM((HEADS_HERE, TOKENS, HEAD_DIM), BF),
        pltpu.VMEM((HEADS_HERE, ALL_ROWS, HEAD_DIM), BF),
        pltpu.VMEM((HEADS_HERE, ALL_ROWS, HEAD_DIM), BF),
        pltpu.VMEM((HEADS_HERE, TOKENS, HEAD_DIM), BF),
        pltpu.VMEM((HEADS_HERE, TOKENS, HEAD_DIM), BF),
        pltpu.VMEM((HEADS_HERE, TOKENS, HEAD_DIM), BF),
        pltpu.VMEM((HEADS_HERE, TOKENS, HEAD_DIM), BF),
        pltpu.VMEM((HEADS_HERE, TOKENS, HEAD_DIM), BF),
        pltpu.VMEM((ALL_ROWS, HEAD_DIM), F32),
        pltpu.VMEM((ALL_ROWS, HEAD_DIM), F32),
        pltpu.VMEM((SEQ, SHARE, SHARE), BF),
        pltpu.VMEM((PROMPT, SHARE), BF),
        pltpu.VMEM((PROMPT, SHARE), F32),
        pltpu.VMEM((SEQ, PROMPT, SHARE), BF),
        pltpu.VMEM((SEQ, PROMPT, SHARE), BF),
        pltpu.VMEM((GROUP, PROMPT + 16, 128), BF),
        pltpu.VMEM((SEQ, GROUP, PROMPT + 16, 128), BF),
        pltpu.VMEM((GROUP * PROMPT, SEQ * 128), BF),
        pltpu.VMEM((SEQ * 128, GROUP * PROMPT), BF),
        pltpu.VMEM((HEADS_HERE, ZS, 128, 256), BF),
        pltpu.VMEM((HEADS_HERE, 2 * PROMPT, 256), F32),
        pltpu.VMEM((HEADS_HERE, 2 * PROMPT, 256), BF),
        pltpu.VMEM((HEADS_HERE, 2 * PROMPT, 256), BF),
        pltpu.VMEM((HEADS_HERE, PROMPT, 256), BF),
        pltpu.VMEM((HEADS_HERE, PROMPT, 256), BF),
        pltpu.VMEM((HEADS_HERE, GROUP, PROMPT, 256), BF),
        pltpu.VMEM((HEADS_HERE, ZS, 128, 256), BF),
        pltpu.VMEM((HEADS_HERE, 4, 128, 256), BF),
        pltpu.VMEM((HEADS_HERE, 4, 128, 256), BF),
        pltpu.VMEM((HEADS_HERE, 2, 128, 256), BF),
        pltpu.VMEM((2, 128, WIDTH), F32),
        pltpu.VMEM((PROMPT, SHARE), BF),
        pltpu.VMEM((1, D_TEXT), F32),
        dma((4, HEADS_HERE)),
        dma((4, HEADS_HERE)),
        dma((4, HEADS_HERE)),
        dma((4, HEADS_HERE)),
        dma((2, HEADS_HERE, ZS)),
        dma((2, HEADS_HERE, ZS)),
        dma((SEQ,)),
        dma((SEQ,)),
        dma((SEQ, 2)),
        dma((2,)),
        dma((GROUP, SEQ)),
        dma((GROUP, SEQ)),
        dma((HEADS_HERE,)),
        dma((HEADS_HERE,)),
        dma((HEADS_HERE,)),
        dma((HEADS_HERE,)),
        dma((HEADS_HERE, 3)),
        dma((HEADS_HERE, 3)),
        dma((HEADS_HERE, 8)),
        dma((HEADS_HERE, 8)),
        dma((2,)),
        dma((2,)),
    ]
    shapes = [tokens] * 4 + [weights] * 2
    made = pl.pallas_call(
        kernel,
        out_shape=shapes,
        in_specs=[smem] + [hbm] * 10,
        out_specs=[hbm] * 6,
        scratch_shapes=scratch,
        name="joint_attention",
        compiler_params=pltpu.CompilerParams(
            collective_id=0, has_side_effects=True, vmem_limit_bytes=56 * 1024 * 1024
        ),
    )(
        prompt_length,
        text_context[0],
        text_gain.reshape(1, D_TEXT),
        text_residual[0],
        text_out_weight,
        key_weight,
        value_weight,
        video_query[0],
        video_key[0],
        video_value[0],
        out_cotangent[0],
    )
    attended, query_grad, key_grad, value_grad, key_weight_grad, value_weight_grad = pl.pallas_call(
        hand_over,
        out_shape=shapes,
        in_specs=[hbm] * 6,
        out_specs=[hbm] * 6,
        scratch_shapes=[pltpu.VMEM(x.shape, x.dtype) for x in shapes] + [dma((2, 6, 2))],
        name="hand_over",
    )(*made)
    return (
        attended[None],
        query_grad[None],
        key_grad[None],
        value_grad[None],
        key_weight_grad,
        value_weight_grad,
    )


def solution(mesh):
    in_specs = (
        P("dp", None, "seq"),
        P("dp", None, None),
        P("seq", None),
        P(),
        P("dp"),
        P("dp", "seq"),
        P("dp", "seq"),
        P("dp", "seq", None),
        P("dp", "seq", None),
        P("dp", "seq", None),
        P("dp", "seq", None),
    )
    out_specs = (
        P("dp", "seq", None),
        P("dp", "seq", None),
        P("dp", "seq", None),
        P("dp", "seq", None),
        P("dp", "seq"),
        P("dp", "seq"),
    )
    return jax.shard_map(body, mesh=mesh, in_specs=in_specs, out_specs=out_specs, check_vma=False)
```

```python
import math

import jax
import jax.numpy as jnp
from jax import lax
from jax.experimental import pallas as pl
from jax.experimental.pallas import tpu as pltpu
from jax.sharding import PartitionSpec as P

MESH = pl.DeviceIdType.MESH
BF = jnp.bfloat16
F32 = jnp.float32

HEAD_DIM = 128
EPSILON = 1e-06
SEQ = 8
ZS = 8
GROUP = 4
HEADS_HERE = 3
ROWS = 128
TOKENS = SEQ * ROWS
PROMPT = 128
ALL_ROWS = TOKENS + PROMPT
D_TEXT = 4096
SHARE = D_TEXT // SEQ
WIDTH = HEADS_HERE * HEAD_DIM
QUERY_BLOCK = 512
EXP2_SCALE = math.log2(math.e) / math.sqrt(HEAD_DIM)
SCALE = 1.0 / math.sqrt(HEAD_DIM)


def nn(left, right):
    return jnp.dot(left, right, preferred_element_type=F32)


def nt(left, right):
    return lax.dot_general(left, right, (((1,), (1,)), ((), ())), preferred_element_type=F32)


def tn(left, right):
    return lax.dot_general(left, right, (((0,), (0,)), ((), ())), preferred_element_type=F32)


def block128(index):
    return pl.ds(pl.multiple_of(index * 128, 128), 128)


def kernel(
    length_ref,
    context_hbm,
    gain_hbm,
    residual,
    out_weight,
    key_weight,
    value_weight,
    video_query,
    video_key,
    video_value,
    out_cotangent,
    attended,
    query_grad,
    key_grad,
    value_grad,
    key_weight_grad,
    value_weight_grad,
    q,
    k,
    v,
    do,
    out,
    dq,
    dk,
    dv,
    dk_total,
    dv_total,
    w_out,
    res,
    summed,
    part,
    part_in,
    piece,
    landed,
    text,
    text_t,
    wkv,
    kv_own,
    kv_core,
    kv_core_in,
    kv_far,
    kv_far_in,
    dkv_all,
    grads,
    grads_in,
    grads_passed,
    grads_sum,
    total_grads,
    context,
    gain,
    in_s,
    in_r,
    out_s,
    out_r,
    w_s,
    w_r,
    rs_s,
    rs_r,
    load_sem,
    res_sem,
    ag_s,
    ag_r,
    kc_s,
    kc_r,
    kf_s,
    kf_r,
    dk_s,
    dk_r,
    wg_s,
    wg_r,
    grad_sem,
    small_sem,
):
    dp = lax.axis_index("dp")
    seq = lax.axis_index("seq")
    y_lo = dp // 16
    z = (dp // 2) % 8
    core = dp % 2

    def seq_of(d):
        return ((seq // 2 + d // 2) % 4) * 2 + (seq % 2 + d % 2) % 2

    def seq_peer(d):
        return (dp, seq_of(d))

    def group_peer(i, d):
        return (((y_lo + i // 2) % 2) * 16 + z * 2 + (core + i % 2) % 2, seq_of(d))

    def core_peer():
        return (dp + 1 - 2 * core, seq)

    def far_peer():
        return ((1 - y_lo) * 16 + z * 2 + core, seq)

    def z_peer(i):
        return (y_lo * 16 + ((z + i) % 8) * 2 + core, seq)

    def remote(src, dst, send, recv, peer):
        return pltpu.make_async_remote_copy(
            src_ref=src, dst_ref=dst, send_sem=send, recv_sem=recv, device_id=peer, device_id_type=MESH
        )

    def loop(low, high, step):
        def run(i, carry):
            step(i)
            return carry

        lax.fori_loop(low, high, run, 0)

    def each(low, high, step):
        for i in range(low, high):
            step(i)


    def w_load(d, half):
        columns = pl.ds(pl.multiple_of(half * 2048 + seq_of(d) * 256, 256), 256)
        return pltpu.make_async_copy(
            out_weight.at[:, columns], w_out.at[d, :, pl.ds(half * 256, 256)], load_sem.at[d, half]
        )

    def res_load(half):
        columns = pl.ds(pl.multiple_of(half * 2048 + seq * 256, 256), 256)
        return pltpu.make_async_copy(
            residual.at[:, columns], res.at[:, pl.ds(half * 256, 256)], res_sem.at[half]
        )

    def weight_copy(n, h, i):
        return remote(
            (key_weight, value_weight)[n].at[:, block128(h)],
            wkv.at[h, z, :, pl.ds(n * 128, 128)],
            w_s.at[n, h, i],
            w_r.at[n, h, i],
            z_peer(i),
        )

    def weight_own(n, h):
        return pltpu.make_async_copy(
            (key_weight, value_weight)[n].at[:, block128(h)],
            wkv.at[h, z, :, pl.ds(n * 128, 128)],
            w_r.at[n, h, 0],
        )

    sources = (video_query, video_key, video_value, out_cotangent)
    landings = (q, k, v, do)
    results = (out, dq, dk, dv)
    targets = (attended, query_grad, key_grad, value_grad)

    def in_copy(n, h, d):
        peer = seq_peer(d)
        return remote(
            sources[n].at[:, block128(peer[1] * HEADS_HERE + h)],
            landings[n].at[h, block128(seq)],
            in_s.at[n, h],
            in_r.at[n, h],
            peer,
        )

    def in_own(n, h):
        return pltpu.make_async_copy(
            sources[n].at[:, block128(seq * HEADS_HERE + h)],
            landings[n].at[h, block128(seq)],
            in_r.at[n, h],
        )

    def out_copy(n, h, d):
        peer = seq_peer(d)
        return remote(
            results[n].at[h, block128(peer[1])],
            targets[n].at[:, block128(seq * HEADS_HERE + h)],
            out_s.at[n, h],
            out_r.at[n, h],
            peer,
        )

    def out_own(n, h):
        return pltpu.make_async_copy(
            results[n].at[h, block128(seq)],
            targets[n].at[:, block128(seq * HEADS_HERE + h)],
            out_r.at[n, h],
        )


    def all_in(n, h):
        rows = landings[n].at[h, pl.ds(0, TOKENS)]
        return pltpu.make_async_copy(rows, rows, in_r.at[n, h])

    def all_in_sent(n, h):
        rows = landings[n].at[h, pl.ds(0, TOKENS - ROWS)]
        return pltpu.make_async_copy(rows, rows, in_s.at[n, h])

    def all_out(n, h):
        rows = results[n].at[h]
        return pltpu.make_async_copy(rows, rows, out_r.at[n, h])

    def all_out_sent(n, h):
        rows = results[n].at[h, pl.ds(0, TOKENS - ROWS)]
        return pltpu.make_async_copy(rows, rows, out_s.at[n, h])

    def part_copy(d):
        return remote(part.at[d], part_in.at[d], rs_s.at[d], rs_r.at[d], seq_peer(d))

    def part_piece(d, c):
        rows = pl.ds(c * 32, 32)
        return remote(part.at[d, rows], part_in.at[d, rows], rs_s.at[d], rs_r.at[d], seq_peer(d))

    def piece_copy(i, d):
        target = ((y_lo + i // 2) % 2) * 2 + (core + i % 2) % 2
        return remote(
            piece.at[target],
            landed.at[seq, (i % 2) * 2 + y_lo],
            ag_s.at[i, d],
            ag_r.at[i, d],
            group_peer(i, d),
        )

    def kv_core_copy(h):
        return remote(kv_core.at[h], kv_core_in.at[h], kc_s.at[h], kc_r.at[h], core_peer())

    def kv_far_copy(h):
        return remote(kv_far.at[h], kv_far_in.at[h], kf_s.at[h], kf_r.at[h], far_peer())

    def dkv_far(h):
        mine = dkv_all.at[h, y_lo]
        return remote(mine, mine, dk_s.at[h, 0], dk_r.at[h, 0], far_peer())

    def dkv_core(h, other):
        side = (1 - y_lo) if other else y_lo
        return remote(
            dkv_all.at[h, side],
            dkv_all.at[h, 2 + side],
            dk_s.at[h, 1 + other],
            dk_r.at[h, 1 + other],
            core_peer(),
        )

    def grad_near(h, n):
        step = (1, ZS - 1)[n]
        return remote(
            grads.at[h, (z + step) % 8], grads_in.at[h, n], wg_s.at[h, n], wg_r.at[h, n], z_peer(step)
        )

    def grad_passed(h, n):
        block, step, low, high = (
            (3, 1, 0, 128),
            (ZS - 3, ZS - 1, 0, 128),
            (4, 2, 0, 64),
            (4, ZS - 2, 64, 128),
        )[n]
        rows = pl.ds(low, high - low)
        return remote(
            grads.at[h, (z + block) % 8, rows],
            grads_passed.at[h, n, rows],
            wg_s.at[h, 2 + n],
            wg_r.at[h, 2 + n],
            z_peer(step),
        )

    def grad_far(h, n):
        step = (2, ZS - 2)[n]
        return remote(
            grads_sum.at[h, n], grads_in.at[h, 2 + n], wg_s.at[h, 6 + n], wg_r.at[h, 6 + n], z_peer(step)
        )

    def send_head_in(h):
        for n in range(4):
            each(1, SEQ, lambda d: in_copy(n, h, d).start())

    def all_group(step):
        each(1, SEQ, lambda d: step(0, d))
        each(1, GROUP, lambda i: each(0, SEQ, lambda d: step(i, d)))


    barrier = pltpu.get_barrier_semaphore()

    def greet(peer):
        pl.semaphore_signal(barrier, inc=1, device_id=peer, device_id_type=MESH)

    all_group(lambda i, d: greet(group_peer(i, d)))
    each(1, ZS, lambda i: greet(z_peer(i)))

    context_load = pltpu.make_async_copy(context_hbm, context, small_sem.at[0])
    gain_load = pltpu.make_async_copy(gain_hbm, gain, small_sem.at[1])
    context_load.start()

    def start_loads(d):
        for half in range(2):
            w_load(d, half).start()

    each(0, SEQ, start_loads)
    for half in range(2):
        res_load(half).start()
    gain_load.start()
    for h in range(HEADS_HERE):
        for n in range(2):
            weight_own(n, h).start()
        for n in range(4):
            in_own(n, h).start()


    def project(d):
        for half in range(2):
            w_load(d, half).wait()
        return nn(context[...], w_out[d])

    context_load.wait()
    gain_load.wait()
    for half in range(2):
        res_load(half).wait()
    summed[...] = project(0) + res[...].astype(F32)

    def project_step(d):
        part[d] = project(d).astype(BF)

    each(1, SEQ, project_step)
    pl.semaphore_wait(barrier, GROUP * SEQ - 1 + ZS - 1)
    for c in range(4):
        each(1, SEQ, lambda d: part_piece(d, c).start())

    def send_weights(h):
        for n in range(2):
            each(1, ZS, lambda i: weight_copy(n, h, i).start())

    send_head_in(0)
    send_weights(0)
    send_weights(1)
    send_weights(2)

    for d in range(1, SEQ):
        part_copy(d).wait_recv()
        summed[...] += part_in[d].astype(F32)
    total = summed[...]
    square = lax.dot_general(
        jnp.ones((16, SHARE), F32),
        total * total,
        (((1,), (1,)), ((), ())),
        precision=lax.Precision.HIGHEST,
        preferred_element_type=F32,
    )
    high = square.astype(BF).astype(F32)
    middle = (square - high).astype(BF).astype(F32)
    low = square - high - middle
    row = lax.broadcasted_iota(jnp.int32, (16, PROMPT), 0)
    square_rows = jnp.where(
        row == 0, high, jnp.where(row == 1, middle, jnp.where(row == 2, low, 0.0))
    ).astype(BF)
    for half in range(2):
        columns = pl.ds(pl.multiple_of(half * 2048 + seq * 256, 256), 256)
        scaled = (total[:, half * 256 : (half + 1) * 256] * gain[:, columns]).astype(BF)
        for c in range(2):
            piece[half * 2 + c, :PROMPT, :] = scaled[:, c * 128 : (c + 1) * 128]
            piece[half * 2 + c, PROMPT:, :] = square_rows
    all_group(lambda i, d: piece_copy(i, d).start())
    landed[seq, y_lo] = piece[y_lo * 2 + core]
    send_head_in(1)


    all_group(lambda i, d: piece_copy(i, d).wait_recv())
    for g in range(GROUP):
        rows = landed[0, g, PROMPT:, :].astype(F32)
        for s in range(1, SEQ):
            rows = rows + landed[s, g, PROMPT:, :].astype(F32)
        mean = jnp.sum(rows, axis=0, keepdims=True) * (1.0 / D_TEXT)
        inverse = lax.rsqrt(jnp.transpose(jnp.broadcast_to(mean, (128, 128))) + EPSILON)
        for s in range(SEQ):
            text[g * 128 : (g + 1) * 128, s * 128 : (s + 1) * 128] = (
                landed[s, g, :PROMPT, :].astype(F32) * inverse
            ).astype(BF)


    def project_kv(h):
        def arrived(i):
            for n in range(2):
                weight_copy(n, h, i).wait_recv()

        each(1, ZS, arrived)
        for n in range(2):
            weight_own(n, h).wait()
        weights = wkv[h].reshape(ZS * 128, 256)
        kv_core[h] = nn(text[256:, :], weights).astype(BF)
        kv_core_copy(h).start()
        kv_own[h] = nn(text[:256, :], weights)

    def add_core(h):
        kv_core_copy(h).wait_recv()
        kv_own[h] += kv_core_in[h].astype(F32)
        kv_far[h] = kv_own[h, block128(1 - y_lo), :].astype(BF)
        kv_far_copy(h).start()

    project_kv(0)

    def next_kv(h):
        project_kv(h)
        add_core(h - 1)

    loop(1, HEADS_HERE, next_kv)
    add_core(HEADS_HERE - 1)
    send_head_in(2)
    for g in range(GROUP):
        text_t[:, g * 128 : (g + 1) * 128] = jnp.transpose(text[g * 128 : (g + 1) * 128, :])


    length = length_ref[0]

    def attend(h, i):
        rows = pl.ds(pl.multiple_of(i * QUERY_BLOCK, QUERY_BLOCK), QUERY_BLOCK)
        queries, cotangent, keys, values = q[h, rows, :], do[h, rows, :], k[h], v[h]
        scores = nt(queries, keys)
        allowed = lax.broadcasted_iota(jnp.int32, (1, PROMPT), 1) < length
        scores = jnp.concatenate(
            [scores[:, :TOKENS], jnp.where(allowed, scores[:, TOKENS:], -jnp.inf)], axis=1
        )
        peak = jnp.max(scores, axis=1, keepdims=True)
        weights = jnp.exp2((scores - peak) * EXP2_SCALE)
        weights_low = weights.astype(BF)
        sums = nn(weights_low, jnp.concatenate([values, jnp.ones_like(values)], axis=1))
        inverse = 1.0 / sums[:, HEAD_DIM:]
        output = sums[:, :HEAD_DIM] * inverse
        out[h, rows, :] = output.astype(BF)
        cotangent_wide = cotangent.astype(F32)
        center = jnp.sum(cotangent_wide * output, axis=1, keepdims=True)
        score_grad = (weights * (nt(cotangent, values) - center)).astype(BF)
        scaled = inverse * SCALE
        dq[h, rows, :] = (nn(score_grad, keys) * scaled).astype(BF)
        dk_total[...] += tn(score_grad, (queries.astype(F32) * scaled).astype(BF))
        dv_total[...] += tn(weights_low, (cotangent_wide * inverse).astype(BF))

    def dkv_forward(h):
        dkv_far(h).wait_recv()
        dkv_core(h, 1).start()

    def weight_grads(h):
        dkv_core(h, 0).wait_recv()
        dkv_core(h, 1).wait_recv()
        products = nn(text_t[...], dkv_all[h].reshape(GROUP * 128, 256))
        grads[h] = products.astype(BF).reshape(ZS, 128, 256)
        for n in range(4):
            grad_passed(h, n).start()
        for n in range(2):
            grad_near(h, n).start()


    def pass_grads(h):
        for n in range(4):
            grad_passed(h, n).wait_recv()
        up = grads[h, (z + 2) % 8].astype(F32) + grads_passed[h, 0].astype(F32)
        grads_sum[h, 0, :64] = (up[:64] + grads_passed[h, 2, :64].astype(F32)).astype(BF)
        grads_sum[h, 0, 64:] = up[64:].astype(BF)
        down = grads[h, (z + ZS - 2) % 8].astype(F32) + grads_passed[h, 1].astype(F32)
        grads_sum[h, 1, :64] = down[:64].astype(BF)
        grads_sum[h, 1, 64:] = (down[64:] + grads_passed[h, 3, 64:].astype(F32)).astype(BF)
        for n in range(2):
            grad_far(h, n).start()

    def send_head_out(h, arrays):
        for n in arrays:
            each(1, SEQ, lambda d: out_copy(n, h, d).start())
            out_own(n, h).start()

    def head(h):
        kv_far_copy(h).wait_recv()
        kv = kv_own[h, block128(y_lo), :] + kv_far_in[h].astype(F32)
        k[h, TOKENS:, :] = kv[:, :128].astype(BF)
        v[h, TOKENS:, :] = kv[:, 128:].astype(BF)
        for n in range(4):
            all_in(n, h).wait()
        dk_total[...] = jnp.zeros_like(dk_total)
        dv_total[...] = jnp.zeros_like(dv_total)
        attend(h, 0)

        @pl.when(h > 0)
        def _():
            dkv_forward(h - 1)

        attend(h, 1)
        dk[h] = dk_total[:TOKENS, :].astype(BF)
        dv[h] = dv_total[:TOKENS, :].astype(BF)
        dkv_all[h, y_lo] = jnp.concatenate(
            [dk_total[TOKENS:, :], dv_total[TOKENS:, :]], axis=1
        ).astype(BF)
        dkv_far(h).start()
        dkv_core(h, 0).start()

        @pl.when(h < HEADS_HERE - 1)
        def _():
            send_head_out(h, range(4))

        @pl.when(h < HEADS_HERE - 2)
        def _():
            send_head_out(h, range(4, 4))

        @pl.when(h > 0)
        def _():
            weight_grads(h - 1)

        @pl.when(h > 1)
        def _():
            pass_grads(h - 2)

    loop(0, HEADS_HERE, head)
    dkv_forward(HEADS_HERE - 1)
    send_head_out(HEADS_HERE - 1, range(4))
    weight_grads(HEADS_HERE - 1)
    pass_grads(HEADS_HERE - 2)
    pass_grads(HEADS_HERE - 1)

    def grads_out(n):
        return pltpu.make_async_copy(
            total_grads.at[n], (key_weight_grad, value_weight_grad)[n], grad_sem.at[n]
        )

    for h in range(HEADS_HERE):
        total = grads[h, z].astype(F32)
        for n in range(2):
            grad_near(h, n).wait_recv()
            grad_far(h, n).wait_recv()
            total = total + grads_in[h, n].astype(F32) + grads_in[h, 2 + n].astype(F32)
        for n in range(2):
            total_grads[n, :, h * 128 : (h + 1) * 128] = total[:, n * 128 : (n + 1) * 128]
    for n in range(2):
        grads_out(n).start()


    def finish(h):
        for n in range(4):
            all_out(n, h).wait()
            all_out_sent(n, h).wait()
            all_in_sent(n, h).wait()
        kv_core_copy(h).wait_send()
        kv_far_copy(h).wait_send()
        dkv_far(h).wait_send()
        dkv_core(h, 0).wait_send()
        dkv_core(h, 1).wait_send()

        for n in range(4):
            grad_passed(h, n).wait_send()
        for n in range(2):
            grad_near(h, n).wait_send()
            grad_far(h, n).wait_send()

        def finish_z(i):
            for n in range(2):
                weight_copy(n, h, i).wait_send()

        each(1, ZS, finish_z)

    loop(0, HEADS_HERE, finish)
    each(1, SEQ, lambda d: part_copy(d).wait_send())
    all_group(lambda i, d: piece_copy(i, d).wait_send())
    for n in range(2):
        grads_out(n).wait()


def hand_over(*refs):
    count = 6
    sources, targets, holds = refs[:count], refs[count : 2 * count], refs[2 * count : 3 * count]
    sem = refs[3 * count]
    parts = [(n, part) for part in range(4) for n in range(count)]

    def load(n, part):
        rows = pl.ds(part * 32, 32)
        return pltpu.make_async_copy(sources[n].at[rows], holds[n].at[rows], sem.at[0, n, part])

    def store(n, part):
        rows = pl.ds(part * 32, 32)
        return pltpu.make_async_copy(holds[n].at[rows], targets[n].at[rows], sem.at[1, n, part])

    for n, part in parts:
        load(n, part).start()
    for n, part in parts:
        load(n, part).wait()
        store(n, part).start()
    for n, part in parts:
        store(n, part).wait()


def body(
    text_context,
    text_residual,
    text_out_weight,
    text_gain,
    prompt_length,
    key_weight,
    value_weight,
    video_query,
    video_key,
    video_value,
    out_cotangent,
):
    hbm = pl.BlockSpec(memory_space=pl.ANY)
    smem = pl.BlockSpec(memory_space=pltpu.SMEM)
    dma = pltpu.SemaphoreType.DMA
    tokens = jax.ShapeDtypeStruct((ROWS, SEQ * WIDTH), BF)
    weights = jax.ShapeDtypeStruct((128, WIDTH), F32)
    scratch = [
        pltpu.VMEM((HEADS_HERE, TOKENS, HEAD_DIM), BF),
        pltpu.VMEM((HEADS_HERE, ALL_ROWS, HEAD_DIM), BF),
        pltpu.VMEM((HEADS_HERE, ALL_ROWS, HEAD_DIM), BF),
        pltpu.VMEM((HEADS_HERE, TOKENS, HEAD_DIM), BF),
        pltpu.VMEM((HEADS_HERE, TOKENS, HEAD_DIM), BF),
        pltpu.VMEM((HEADS_HERE, TOKENS, HEAD_DIM), BF),
        pltpu.VMEM((HEADS_HERE, TOKENS, HEAD_DIM), BF),
        pltpu.VMEM((HEADS_HERE, TOKENS, HEAD_DIM), BF),
        pltpu.VMEM((ALL_ROWS, HEAD_DIM), F32),
        pltpu.VMEM((ALL_ROWS, HEAD_DIM), F32),
        pltpu.VMEM((SEQ, SHARE, SHARE), BF),
        pltpu.VMEM((PROMPT, SHARE), BF),
        pltpu.VMEM((PROMPT, SHARE), F32),
        pltpu.VMEM((SEQ, PROMPT, SHARE), BF),
        pltpu.VMEM((SEQ, PROMPT, SHARE), BF),
        pltpu.VMEM((GROUP, PROMPT + 16, 128), BF),
        pltpu.VMEM((SEQ, GROUP, PROMPT + 16, 128), BF),
        pltpu.VMEM((GROUP * PROMPT, SEQ * 128), BF),
        pltpu.VMEM((SEQ * 128, GROUP * PROMPT), BF),
        pltpu.VMEM((HEADS_HERE, ZS, 128, 256), BF),
        pltpu.VMEM((HEADS_HERE, 2 * PROMPT, 256), F32),
        pltpu.VMEM((HEADS_HERE, 2 * PROMPT, 256), BF),
        pltpu.VMEM((HEADS_HERE, 2 * PROMPT, 256), BF),
        pltpu.VMEM((HEADS_HERE, PROMPT, 256), BF),
        pltpu.VMEM((HEADS_HERE, PROMPT, 256), BF),
        pltpu.VMEM((HEADS_HERE, GROUP, PROMPT, 256), BF),
        pltpu.VMEM((HEADS_HERE, ZS, 128, 256), BF),
        pltpu.VMEM((HEADS_HERE, 4, 128, 256), BF),
        pltpu.VMEM((HEADS_HERE, 4, 128, 256), BF),
        pltpu.VMEM((HEADS_HERE, 2, 128, 256), BF),
        pltpu.VMEM((2, 128, WIDTH), F32),
        pltpu.VMEM((PROMPT, SHARE), BF),
        pltpu.VMEM((1, D_TEXT), F32),
        dma((4, HEADS_HERE)),
        dma((4, HEADS_HERE)),
        dma((4, HEADS_HERE)),
        dma((4, HEADS_HERE)),
        dma((2, HEADS_HERE, ZS)),
        dma((2, HEADS_HERE, ZS)),
        dma((SEQ,)),
        dma((SEQ,)),
        dma((SEQ, 2)),
        dma((2,)),
        dma((GROUP, SEQ)),
        dma((GROUP, SEQ)),
        dma((HEADS_HERE,)),
        dma((HEADS_HERE,)),
        dma((HEADS_HERE,)),
        dma((HEADS_HERE,)),
        dma((HEADS_HERE, 3)),
        dma((HEADS_HERE, 3)),
        dma((HEADS_HERE, 8)),
        dma((HEADS_HERE, 8)),
        dma((2,)),
        dma((2,)),
    ]
    shapes = [tokens] * 4 + [weights] * 2
    made = pl.pallas_call(
        kernel,
        out_shape=shapes,
        in_specs=[smem] + [hbm] * 10,
        out_specs=[hbm] * 6,
        scratch_shapes=scratch,
        name="joint_attention",
        compiler_params=pltpu.CompilerParams(
            collective_id=0, has_side_effects=True, vmem_limit_bytes=56 * 1024 * 1024
        ),
    )(
        prompt_length,
        text_context[0],
        text_gain.reshape(1, D_TEXT),
        text_residual[0],
        text_out_weight,
        key_weight,
        value_weight,
        video_query[0],
        video_key[0],
        video_value[0],
        out_cotangent[0],
    )
    attended, query_grad, key_grad, value_grad, key_weight_grad, value_weight_grad = pl.pallas_call(
        hand_over,
        out_shape=shapes,
        in_specs=[hbm] * 6,
        out_specs=[hbm] * 6,
        scratch_shapes=[pltpu.VMEM(x.shape, x.dtype) for x in shapes] + [dma((2, 6, 4))],
        name="hand_over",
    )(*made)
    return (
        attended[None],
        query_grad[None],
        key_grad[None],
        value_grad[None],
        key_weight_grad,
        value_weight_grad,
    )


def solution(mesh):
    in_specs = (
        P("dp", None, "seq"),
        P("dp", None, None),
        P("seq", None),
        P(),
        P("dp"),
        P("dp", "seq"),
        P("dp", "seq"),
        P("dp", "seq", None),
        P("dp", "seq", None),
        P("dp", "seq", None),
        P("dp", "seq", None),
    )
    out_specs = (
        P("dp", "seq", None),
        P("dp", "seq", None),
        P("dp", "seq", None),
        P("dp", "seq", None),
        P("dp", "seq"),
        P("dp", "seq"),
    )
    return jax.shard_map(body, mesh=mesh, in_specs=in_specs, out_specs=out_specs, check_vma=False)
```
